32 devices in a mesh: prow: 4 (over x, core), pcol: 8 (over z, y).
Axes of the slice: x: 2, y: 2, z: 4, core: 2. Of those that a mesh axis runs over, the one named last changes fastest.
Arguments:
- factor: bfloat16 [8, 4, 4, 8, 256, 256], P(None, 'prow', None, 'pcol')
- right_side: bfloat16 [4, 8, 256, 256], P(None, 'pcol'), may hold values from -6 to 6
- node_blocks: int32 [15], replicated, may hold values from 1 to 8, as said below
- front_mask: int32 [15, 32], replicated, may hold values from 0 to 1, as said below
Outputs:
- solution: bfloat16 [4, 8, 256, 256], P(None, 'pcol')
The draws below stay inside these ranges and needn't reach their ends.
Inputs may be any that keep to these rules, and one draw needn't show every extreme that they name: node_blocks[s] counts the blocks of node s of a complete binary elimination tree in heap order (the parent of s is (s - 1) // 2); the nodes of one depth together have 8 blocks. front_mask[s, i] is 1 only where block i belongs to a strict ancestor of node s.
All inputs are finite; a program needn't handle non-finite values.
Results may differ from the reference program's by a relative error of at most 0.024.
Values may be sent and summed in bfloat16 or wider, within the bound.
A program may use at most 128 MiB of HBM per device.

```python
import math
import jax
import jax.numpy as jnp
import numpy as np
from jax import lax

LEVELS = 4
BS = 256
NRHS = 256
K = 8
NB = 32
NODES = 15
N_PROW = 4
N_PCOL = 8


def node_order_drawn():
    ordering = []
    for depth_now in range(LEVELS - 1, -1, -1):
        ordering.extend(range(2 ** depth_now - 1, 2 ** (depth_now + 1) - 1))
    return ordering


def node_table_drawn(node_blocks, total_blocks):
    node_count = node_blocks.shape[0]
    ordered = jnp.array(node_order_drawn(), dtype=jnp.int32)
    node_ids = jnp.arange(node_count, dtype=jnp.int32)
    pick_sizes = (ordered[:, None] == node_ids[None, :]).astype(jnp.int32)
    level_sizes = jnp.sum(pick_sizes * node_blocks[None, :], axis=1).astype(jnp.int32)
    block_ends = jnp.cumsum(level_sizes).astype(jnp.int32)
    block_ids = jnp.arange(total_blocks, dtype=jnp.int32)
    positions = jnp.sum((block_ids[:, None] >= block_ends[None, :]).astype(jnp.int32), axis=1).astype(jnp.int32)
    return jnp.sum((positions[:, None] == node_ids[None, :]).astype(jnp.int32) * ordered[None, :], axis=1).astype(jnp.int32)


def tree_sizes(key):
    sizes_key = jax.random.fold_in(key, 11)
    pieces_list = [jnp.full((1,), K, jnp.int32)]
    for depth_now in range(1, LEVELS):
        node_count = 2 ** depth_now
        level_key = jax.random.fold_in(sizes_key, depth_now)
        cut_points = jnp.sort(jax.random.permutation(level_key, K - 1)[:node_count - 1] + 1).astype(jnp.int32)
        boundaries = jnp.concatenate([jnp.zeros((1,), jnp.int32), cut_points, jnp.full((1,), K, jnp.int32)])
        pieces_list.append(boundaries[1:] - boundaries[:-1])
    return jnp.concatenate(pieces_list).astype(jnp.int32)


def ancestor_table():
    table_rows = []
    for node_now in range(NODES):
        ancestor_marks = [0] * NODES
        walker = node_now
        while walker > 0:
            walker = (walker - 1) // 2
            ancestor_marks[walker] = 1
        table_rows.append(ancestor_marks)
    return np.array(table_rows, dtype=np.int32)


def draw_node_blocks(key, part):
    return tree_sizes(key)


def draw_front_mask(key, part):
    block_node = node_table_drawn(tree_sizes(key), NB)
    ancestors = jnp.asarray(ancestor_table())
    node_ids = jnp.arange(NODES, dtype=jnp.int32)
    onehot_nodes = (block_node[:, None] == node_ids[None, :]).astype(jnp.int32)
    ancestor_blocks = jnp.sum(ancestors[:, None, :] * onehot_nodes[None, :, :], axis=2)
    coins = jax.random.randint(jax.random.fold_in(key, 23), (NODES, NB), 0, 4)
    return (ancestor_blocks * (coins < 3).astype(jnp.int32)).astype(jnp.int32)


def draw_factor(key, part):
    spread = 0.7 / math.sqrt(K * BS)
    full_shape = (NB, NB, BS, BS)
    entries = jax.random.normal(key, full_shape, jnp.float32) * spread
    same_block = (jnp.arange(NB)[:, None] == jnp.arange(NB)[None, :]).astype(jnp.float32)
    entries = entries + same_block[:, :, None, None] * jnp.eye(BS, dtype=jnp.float32)[None, None, :, :]
    return entries.reshape(NB // N_PROW, N_PROW, NB // N_PCOL, N_PCOL, BS, BS).astype(jnp.bfloat16)


def level_of(own_key, extent, cuts, least, top_value):
    def one(position, parts):
        heights = jax.random.uniform(jax.random.fold_in(jax.random.fold_in(own_key, 6), position), (parts,), jnp.float32, least / len(cuts), top_value / len(cuts))
        return jnp.repeat(jnp.exp(heights), extent[position] // parts).reshape((-1,) + (1,) * (len(extent) - position - 1))

    level = one(*cuts[0])
    for cut in cuts[1:]:
        level = level * one(*cut)
    return level


def gaussian(key, shape, scale, bound, pieces=(), kind=jnp.bfloat16):
    result = jax.random.normal(key, shape, jnp.float32) * scale
    if len(pieces) > 0:
        result = level_of(key, shape, pieces, -0.22, 0.18) * result
    return jnp.clip(result, min=-bound, max=bound).astype(kind)


def setup_inputs(seed: int = 0) -> dict:
    key_list = jax.random.split(jax.random.key(seed), 5)
    factor = draw_factor(jax.random.fold_in(key_list[4], 71), 0)
    right_side = gaussian(key_list[1], (NB // N_PCOL, N_PCOL, BS, NRHS), 1.0, 6.0, ((1, 8),))
    node_blocks = draw_node_blocks(jax.random.fold_in(key_list[4], 71), 0)
    front_mask = draw_front_mask(jax.random.fold_in(key_list[4], 71), 0)
    return {"factor": factor, "right_side": right_side, "node_blocks": node_blocks, "front_mask": front_mask}


def node_order():
    ordering = []
    for depth_now in range(LEVELS - 1, -1, -1):
        ordering.extend(range(2 ** depth_now - 1, 2 ** (depth_now + 1) - 1))
    return ordering


def node_table(node_blocks, total_blocks):
    node_count = node_blocks.shape[0]
    ordered = jnp.array(node_order(), dtype=jnp.int32)
    node_ids = jnp.arange(node_count, dtype=jnp.int32)
    pick_sizes = (ordered[:, None] == node_ids[None, :]).astype(jnp.int32)
    level_sizes = jnp.sum(pick_sizes * node_blocks[None, :], axis=1).astype(jnp.int32)
    block_ends = jnp.cumsum(level_sizes).astype(jnp.int32)
    block_ids = jnp.arange(total_blocks, dtype=jnp.int32)
    positions = jnp.sum((block_ids[:, None] >= block_ends[None, :]).astype(jnp.int32), axis=1).astype(jnp.int32)
    return jnp.sum((positions[:, None] == node_ids[None, :]).astype(jnp.int32) * ordered[None, :], axis=1).astype(jnp.int32)


def reference(factor, right_side, node_blocks, front_mask):
    blocks = factor.reshape(NB, NB, BS, BS)
    vectors = right_side.reshape(NB, BS, NRHS)
    block_node = node_table(node_blocks, NB)
    block_ids = jnp.arange(NB, dtype=jnp.int32)
    front_full = jnp.transpose(front_mask[block_node])
    diag_full = (block_node[:, None] == block_node[None, :]) & (block_ids[:, None] >= block_ids[None, :])
    solved = jnp.zeros((NB, BS, NRHS), jnp.bfloat16)
    for section_now in range(LEVELS):
        first_row = section_now * K
        after_row = first_row + K
        rows_now = jnp.arange(first_row, after_row, dtype=jnp.int32)
        if section_now == 0:
            rhs_now = vectors[first_row:after_row]
        else:
            earlier = solved[:first_row].reshape(section_now, K, BS, NRHS).astype(jnp.float32)

            def update_row(row_id):
                tile_set = blocks[row_id, :first_row].reshape(section_now, K, BS, BS).astype(jnp.float32)
                live_bits = front_full[row_id, :first_row].reshape(section_now, K).astype(jnp.float32)
                per_column = jnp.einsum("hcxy,hcyn->cxn", tile_set * live_bits[:, :, None, None], earlier, precision=lax.Precision.HIGHEST)
                rounded = lax.optimization_barrier(per_column.astype(jnp.bfloat16))
                return jnp.sum(rounded.astype(jnp.float32), axis=0)

            update = lax.map(update_row, rows_now)
            rhs_now = (vectors[first_row:after_row].astype(jnp.float32) - update).astype(jnp.bfloat16)
        rhs_float = rhs_now.astype(jnp.float32)

        def solve_row(row_id):
            tile_set = blocks[row_id, first_row:after_row].astype(jnp.float32)
            live_bits = diag_full[row_id, first_row:after_row].astype(jnp.float32)
            diag_terms = jnp.einsum("cxy,cyn->cxn", tile_set * live_bits[:, None, None], rhs_float, precision=lax.Precision.HIGHEST)
            rounded = lax.optimization_barrier(diag_terms.astype(jnp.bfloat16))
            return jnp.sum(rounded.astype(jnp.float32), axis=0).astype(jnp.bfloat16)

        solved = solved.at[first_row:after_row].set(lax.map(solve_row, rows_now))
    return solved.reshape(NB // N_PCOL, N_PCOL, BS, NRHS)
```

```python
import functools

import jax
import jax.numpy as jnp
from jax import lax
from jax.experimental import pallas as pl
from jax.experimental.pallas import tpu as pltpu
from jax.sharding import PartitionSpec as P

MESH = pl.DeviceIdType.MESH
LANES = 128


def kernel(
    n_prow, n_pcol, factor, right, nodes, front, out,
    tiles, acc, parts, inbox, vec, load_sem, send_parts, recv_parts, send_vec, recv_vec,
):
    levels = right.shape[0]
    per_level = n_pcol // n_prow
    strip = vec.shape[3]
    chunks = vec.shape[1]
    size = strip * n_prow
    pr = lax.axis_index("prow")
    pc = lax.axis_index("pcol")

    def device(row, col):
        return {"prow": row, "pcol": col}

    barrier = pltpu.get_barrier_semaphore()
    home = lax.rem(pc, n_prow)
    for k in range(n_pcol):
        if k == 0:
            @pl.when(home != pr)
            def _():
                pl.semaphore_signal(barrier, inc=1, device_id=device(home, pc), device_id_type=MESH)
        else:
            source = lax.rem(pc + k, n_pcol)
            pl.semaphore_signal(barrier, inc=1, device_id=device(home, source), device_id_type=MESH)
    for k in range(1, n_prow):
        pl.semaphore_signal(
            barrier, inc=1, device_id=device(lax.rem(pr + k, n_prow), pc), device_id_type=MESH
        )

    loads = {}
    for g in range(levels):
        for h in range(g, -1, -1):
            loads[g, h] = pltpu.make_async_copy(
                factor.at[pl.ds(per_level * g, per_level), 0, h, 0],
                tiles.at[h, pl.ds(per_level * g, per_level)],
                load_sem.at[g, h],
            )
    loads[0, 0].start()
    for key in loads:
        if key != (0, 0):
            loads[key].start()

    ends = []
    for g in range(levels):
        first = 2 ** (levels - 1 - g) - 1
        total, ends_now = jnp.int32(0), []
        for k in range(first + 1):
            total = total + nodes[first + k]
            ends_now.append(total)
        ends.append(ends_now)

    def node(g, place):
        found = jnp.int32(2 ** (levels - 1 - g) - 1)
        for end in ends[g][:-1]:
            found = found + jnp.where(place >= end, 1, 0)
        return found

    col_node = [node(g, pc) for g in range(levels)]

    def row_place(r):
        return r * n_prow + pr

    def diag_bit(g, r):
        place = row_place(r)
        return jnp.where((node(g, place) == col_node[g]) & (place >= pc), 1.0, 0.0).astype(jnp.float32)

    def front_bit(g, h, r):
        return front[col_node[h], g * n_pcol + row_place(r)].astype(jnp.float32)

    def lanes(ch):
        return pl.ds(ch * LANES, LANES)

    order = [lax.rem(pc // n_prow + 1 + k, per_level) for k in range(per_level)]

    def part_copies(p, ch, r):
        place = row_place(r)
        copies = []
        for k in range(n_prow):
            s = lax.rem(pr + k, n_prow)
            copies.append(pltpu.make_async_remote_copy(
                src_ref=parts.at[p % 2, ch, r, s],
                dst_ref=inbox.at[p, ch, pc],
                send_sem=send_parts.at[p % 2, ch, r, s],
                recv_sem=recv_parts.at[p, ch, pc],
                device_id=device(s, place),
                device_id_type=MESH,
            ))
        return copies

    def guarded(p, r, action):
        if p % 2 == 0:
            pl.when(row_place(r) >= pc)(action)
        else:
            action()

    def send(p, ch, r):
        def go():
            for k, copy in enumerate(part_copies(p, ch, r)):
                if k == 0:
                    @pl.when(row_place(r) == pc)
                    def _():
                        pltpu.make_async_copy(
                            parts.at[p % 2, ch, r, pr], inbox.at[p, ch, pc], recv_parts.at[p, ch, pc]
                        ).start()
                    pl.when(row_place(r) != pc)(copy.start)
                else:
                    copy.start()
        guarded(p, r, go)

    def finish_sends(p, ch):
        for r in order:
            def go(r=r):
                for k, copy in enumerate(part_copies(p, ch, r)):
                    if k == 0:
                        pl.when(row_place(r) != pc)(copy.wait_send)
                    else:
                        copy.wait_send()
            guarded(p, r, go)
        for copy in vec_copies(p, ch):
            copy.wait_send()

    def vec_copies(p, ch):
        copies = []
        for k in range(1, n_prow):
            s = lax.rem(pr + k, n_prow)
            copies.append(pltpu.make_async_remote_copy(
                src_ref=vec.at[p, ch, pr],
                dst_ref=vec.at[p, ch, pr],
                send_sem=send_vec.at[p % 2, ch, s],
                recv_sem=recv_vec.at[p, ch, pr],
                device_id=device(s, pc),
                device_id_type=MESH,
            ))
        return copies

    def reduce_and_share(p, ch):
        def add(source, total):
            slot = inbox.at[p, ch, source]
            pltpu.make_async_remote_copy(
                src_ref=slot, dst_ref=slot, send_sem=send_vec.at[0, 0, 0],
                recv_sem=recv_parts.at[p, ch, source], device_id=device(pr, pc), device_id_type=MESH,
            ).wait_recv()
            return total + inbox[p, ch, source].astype(jnp.float32)

        total = jnp.zeros((strip, LANES), jnp.float32)
        if p % 2 == 0:
            total = lax.fori_loop(0, pc + 1, add, total)
        else:
            total = lax.fori_loop(0, n_pcol, add, total)
            rows = pl.ds(pl.multiple_of(pr * strip, strip), strip)
            total = right[(p + 1) // 2, 0, rows, lanes(ch)].astype(jnp.float32) - total
        vec[p, ch, pr] = total.astype(jnp.bfloat16)
        for copy in vec_copies(p, ch):
            copy.start()

    def receive(p, ch):
        for k in range(1, n_prow):
            s = lax.rem(pr + k, n_prow)
            slot = vec.at[p, ch, s]
            pltpu.make_async_remote_copy(
                src_ref=slot, dst_ref=slot, send_sem=send_vec.at[0, 0, 0],
                recv_sem=recv_vec.at[p, ch, s], device_id=device(pr, pc), device_id_type=MESH,
            ).wait_recv()
        return vec[p, ch].reshape(size, LANES)

    def product(g, h, r, x):
        return jnp.dot(tiles[h, per_level * g + r], x, preferred_element_type=jnp.float32)

    def put(p, ch, r, value):
        parts[p % 2, ch, r] = value.astype(jnp.bfloat16).reshape(n_prow, strip, LANES)
        send(p, ch, r)

    phases = 2 * levels - 1
    loads[0, 0].wait()
    for p in range(phases + 1):
        g = (p + 1) // 2
        values = []
        for ch in range(chunks):
            x = right[0, 0, :, lanes(ch)] if p == 0 else receive(p - 1, ch)
            values.append(x)
            if p % 2 == 1:
                out[g - 1, 0, :, lanes(ch)] = x
            if p == phases:
                continue
            if ch == 0 and p > 0:
                for h in ([g] if p % 2 == 0 else range(g)):
                    if p % 2 == 0 or h == g - 1:
                        loads[g, h].wait()
            for k, r in enumerate(order):
                if p % 2 == 0:
                    value = product(g, g, r, x) * diag_bit(g, r)
                else:
                    value = product(g, g - 1, r, x) * front_bit(g, g - 1, r)
                    if g > 1:
                        value = value + acc[g, ch, r]
                if p == 0 and ch == 0 and k == 0:
                    pl.semaphore_wait(barrier, n_pcol + n_prow - 2 + jnp.where(home != pr, 1, 0))
                put(p, ch, r, value)
        if p > 0:
            for ch in range(chunks):
                finish_sends(p - 1, ch)
        if p == phases:
            break
        if p % 2 == 1:
            h = g - 1
            for later in range(g + 1, levels):
                loads[later, h].wait()
                for ch in range(chunks):
                    for r in range(per_level):
                        value = product(later, h, r, values[ch]) * front_bit(later, h, r)
                        acc[later, ch, r] = value if h == 0 else acc[later, ch, r] + value
        for ch in range(chunks):
            reduce_and_share(p, ch)


def local(n_prow, n_pcol, factor, right_side, node_blocks, front_mask):
    levels, _, size, width = right_side.shape
    per_level = n_pcol // n_prow
    strip = size // n_prow
    chunks = width // LANES
    phases = 2 * levels - 1
    vmem = pl.BlockSpec(memory_space=pltpu.VMEM)
    smem = pl.BlockSpec(memory_space=pltpu.SMEM)
    dma = pltpu.SemaphoreType.DMA
    return pl.pallas_call(
        functools.partial(kernel, n_prow, n_pcol),
        out_shape=jax.ShapeDtypeStruct(right_side.shape, jnp.bfloat16),
        in_specs=[pl.BlockSpec(memory_space=pl.ANY), vmem, smem, smem],
        out_specs=vmem,
        scratch_shapes=[
            pltpu.VMEM((levels, levels * per_level, size, size), jnp.bfloat16),
            pltpu.VMEM((levels, chunks, per_level, size, LANES), jnp.float32),
            pltpu.VMEM((2, chunks, per_level, n_prow, strip, LANES), jnp.bfloat16),
            pltpu.VMEM((phases, chunks, n_pcol, strip, LANES), jnp.bfloat16),
            pltpu.VMEM((phases, chunks, n_prow, strip, LANES), jnp.bfloat16),
            dma((levels, levels)),
            dma((2, chunks, per_level, n_prow)),
            dma((phases, chunks, n_pcol)),
            dma((2, chunks, n_prow)),
            dma((phases, chunks, n_prow)),
        ],
        compiler_params=pltpu.CompilerParams(
            collective_id=0, has_side_effects=True, vmem_limit_bytes=40 * 2**20
        ),
    )(factor, right_side, node_blocks, front_mask)


def solution(mesh):
    in_specs = (P(None, "prow", None, "pcol", None, None), P(None, "pcol", None, None), P(), P())
    out_specs = P(None, "pcol", None, None)
    return jax.shard_map(
        functools.partial(local, mesh.shape["prow"], mesh.shape["pcol"]),
        mesh=mesh, in_specs=in_specs, out_specs=out_specs, check_vma=False,
    )
```

```python
import functools

import jax
import jax.numpy as jnp
from jax import lax
from jax.experimental import pallas as pl
from jax.experimental.pallas import tpu as pltpu
from jax.sharding import PartitionSpec as P

MESH = pl.DeviceIdType.MESH
CHUNKS = 2


def pair(g, h):
    return g * (g + 1) // 2 + h


def dot_nt(a, b):
    return lax.dot_general(a, b, (((1,), (1,)), ((), ())), preferred_element_type=jnp.float32)


def kernel(
    n_prow, n_pcol, factor, right, nodes, front, out,
    tiles, flat, turned, acc, first, parts, inbox, solved,
    load_sem, flat_sem, tile_send, relay_send, tile_recv,
    first_send, part_send, part_recv, share_send, share_recv,
):
    levels, _, size, width = right.shape
    per_level = n_pcol // n_prow
    rows = width // n_prow // CHUNKS
    pairs = n_prow // 2 - 1
    phases = 2 * levels - 1
    pr = lax.axis_index("prow")
    pc = lax.axis_index("pcol")
    near = pr + 1 - 2 * lax.rem(pr, 2)

    def device(row, col):
        return {"prow": row, "pcol": col}

    def remote(src, dst, send, recv, row, col):
        return pltpu.make_async_remote_copy(
            src_ref=src, dst_ref=dst, send_sem=send, recv_sem=recv,
            device_id=device(row, col), device_id_type=MESH,
        )

    def arrived(slot, sem):
        remote(slot, slot, share_send.at[0, 0, 0], sem, pr, pc).wait_recv()

    barrier = pltpu.get_barrier_semaphore()
    home = lax.rem(pc, n_prow)

    def greet(row, col):
        pl.semaphore_signal(barrier, inc=1, device_id=device(row, col), device_id_type=MESH)

    for k in range(1, n_prow):
        greet(lax.rem(pr + k, n_prow), pc)
    for k in range(1, n_pcol):
        greet(pr, lax.rem(pc + k, n_pcol))

    @pl.when(home != pr)
    def _():
        for k in range(n_pcol):
            greet(home, lax.rem(pc + k, n_pcol))

    def place(r):
        return r * n_prow + pr

    def load(g, h, r):
        return pltpu.make_async_copy(
            factor.at[per_level * g + r, 0, h, 0], tiles.at[pair(g, h), place(r)],
            load_sem.at[pair(g, h), r],
        )

    flat_copy = pltpu.make_async_copy(right.at[:, 0], flat, flat_sem)
    flat_copy.start()
    for g in range(levels):
        for h in range(g + 1):
            for r in range(per_level):
                load(g, h, r).start()

    ends = []
    for g in range(levels):
        base = 2 ** (levels - 1 - g) - 1
        total, ends_now = jnp.int32(0), []
        for k in range(base + 1):
            total = total + nodes[base + k]
            ends_now.append(total)
        ends.append(ends_now)

    def node(g, i):
        found = jnp.int32(2 ** (levels - 1 - g) - 1)
        for end in ends[g][:-1]:
            found = found + jnp.where(i >= end, 1, 0)
        return found

    col_node = [node(g, pc) for g in range(levels)]

    def diag_bit(g, i):
        return jnp.where((node(g, i) == col_node[g]) & (i >= pc), 1.0, 0.0).astype(jnp.float32)

    def front_bit(g, h, i):
        return front[col_node[h], g * n_pcol + i].astype(jnp.float32)

    def live(g, h, i, action):
        if g == h:
            pl.when(i >= pc)(action)
        else:
            action()

    def tile_copies(g, h, r):
        q, i = pair(g, h), place(r)
        targets = [lax.rem(pr + 2 * k, n_prow) for k in range(1, pairs + 1)] + [near]
        return [
            remote(factor.at[per_level * g + r, 0, h, 0], tiles.at[q, i],
                   tile_send.at[q, r, k], tile_recv.at[q, i], target, pc)
            for k, target in enumerate(targets)
        ]

    def relay_copies(g, h, r):
        q = pair(g, h)
        copies = []
        for k in range(1, pairs + 1):
            i = r * n_prow + lax.rem(pr + 2 * k, n_prow)
            copies.append((i, remote(tiles.at[q, i], tiles.at[q, i], relay_send.at[q, r, k - 1],
                                     tile_recv.at[q, i], near, pc)))
        return copies

    def issue(g, h):
        for r in range(per_level):
            def go(r=r):
                for copy in tile_copies(g, h, r):
                    copy.start()
            live(g, h, place(r), go)

    def relay(g, h):
        for r in range(per_level):
            for i, copy in relay_copies(g, h, r):
                def go(i=i, copy=copy):
                    arrived(tiles.at[pair(g, h), i], tile_recv.at[pair(g, h), i])
                    copy.start()
                live(g, h, i, go)

    def collect(g, h):
        q = pair(g, h)
        for r in range(per_level):
            load(g, h, r).wait()
            for k in range(pairs + 1):
                i = r * n_prow + lax.rem(near + 2 * k, n_prow)
                live(g, h, i, lambda i=i: arrived(tiles.at[q, i], tile_recv.at[q, i]))

    def settle(g, h):
        for r in range(per_level):
            def go(r=r):
                for copy in tile_copies(g, h, r):
                    copy.wait_send()
            live(g, h, place(r), go)
            for i, copy in relay_copies(g, h, r):
                live(g, h, i, copy.wait_send)

    def first_copies(r, ch):
        return [
            remote(first.at[r, s, ch], inbox.at[0, ch, pc], first_send.at[r, s, ch],
                   part_recv.at[0, ch, pc], s, place(r))
            for s in [lax.rem(pr + k, n_prow) for k in range(n_prow)]
        ]

    def first_each(r, ch, action, stay):
        for k, copy in enumerate(first_copies(r, ch)):
            if k == 0:
                pl.when(place(r) != pc)(lambda: action(copy))
                if stay is not None:
                    pl.when(place(r) == pc)(stay)
            else:
                action(copy)

    far = [lax.rem(pc // n_prow + 1 + k, per_level) for k in range(per_level)]

    def first_phase():
        for r in far:
            i = place(r)

            @pl.when(i >= pc)
            def _():
                value = dot_nt(turned[0], tiles[0, i]) * diag_bit(0, i)
                first[r] = value.astype(jnp.bfloat16).reshape(n_prow, CHUNKS, rows, size)
                for ch in range(CHUNKS):
                    def stay(ch=ch):
                        inbox[0, ch, pc] = first[r, pr, ch]
                    first_each(r, ch, lambda copy: copy.start(), stay)

    def first_settle():
        for r in far:
            @pl.when(place(r) >= pc)
            def _():
                for ch in range(CHUNKS):
                    first_each(r, ch, lambda copy: copy.wait_send(), None)

    def part_copy(p, ch, i):
        return remote(parts.at[p % 2, ch, i], inbox.at[p, ch, pc], part_send.at[p % 2, ch, i],
                      part_recv.at[p, ch, pc], pr, i)

    def each_row(body):
        def step(k):
            return lax.rem(pc + n_pcol // 2 + k, n_pcol)

        if n_pcol <= 8:
            for k in range(n_pcol):
                if k != n_pcol // 2:
                    body(step(k))
        else:
            def loop(k, carry):
                i = step(k)
                pl.when(i != pc)(lambda: body(i))
                return carry

            lax.fori_loop(0, n_pcol, loop, 0)

    def products(p, ch, x):
        g = (p + 1) // 2
        h = g if p % 2 == 0 else g - 1

        def result(i):
            value = dot_nt(x, tiles[pair(g, h), i])
            if p % 2 == 0:
                return value * diag_bit(g, i)
            value = value * front_bit(g, h, i)
            return value + acc[g, ch, i] if g > 1 else value

        def body(i):
            def go():
                parts[p % 2, ch, i] = result(i).astype(jnp.bfloat16)
                part_copy(p, ch, i).start()
            live(g, h, i, go)

        each_row(body)
        inbox[p, ch, pc] = result(pc).astype(jnp.bfloat16)

    def finish(p):
        if p == 0:
            return first_settle()
        g = (p + 1) // 2
        h = g if p % 2 == 0 else g - 1
        for ch in range(CHUNKS):
            each_row(lambda i: live(g, h, i, lambda: part_copy(p, ch, i).wait_send()))

    def later(g, h):
        for ch in range(CHUNKS):
            x = solved[h, pr, ch]

            def body(i):
                value = dot_nt(x, tiles[pair(g, h), i]) * front_bit(g, h, i)
                acc[g, ch, i] = value if h == 0 else acc[g, ch, i] + value

            each_row(body)
            body(pc)

    def share_copies(g, ch):
        return [
            remote(solved.at[g, pr, ch], solved.at[g, pr, ch], share_send.at[g, ch, s],
                   share_recv.at[g, ch, pr], s, pc)
            for s in [lax.rem(pr + k, n_prow) for k in range(1, n_prow)]
        ]

    def reduce(p, ch):
        def add(source, total):
            own = source == pc
            if p == 0:
                own = own & (home == pr)
            pl.when(jnp.logical_not(own))(
                lambda: arrived(inbox.at[p, ch, source], part_recv.at[p, ch, source])
            )
            return total + inbox[p, ch, source].astype(jnp.float32)

        total = jnp.zeros((rows, size), jnp.float32)
        g = (p + 1) // 2
        if p % 2 == 0:
            x = lax.fori_loop(0, pc + 1, add, total).astype(jnp.bfloat16)
            solved[g, pr, ch] = x
            for copy in share_copies(g, ch):
                copy.start()
            return x
        total = lax.fori_loop(0, n_pcol, add, total)
        start = pl.multiple_of((pr * CHUNKS + ch) * rows, rows)
        return (turned[g, pl.ds(start, rows), :].astype(jnp.float32) - total).astype(jnp.bfloat16)

    def write(g):
        for ch in range(CHUNKS):
            for k in range(1, n_prow):
                s = lax.rem(pr + k, n_prow)
                arrived(solved.at[g, s, ch], share_recv.at[g, ch, s])
        out[g, 0] = solved[g].reshape(width, size).astype(jnp.float32).T.astype(jnp.bfloat16)
        for ch in range(CHUNKS):
            for copy in share_copies(g, ch):
                copy.wait_send()

    def turn(g):
        turned[g] = flat[g].astype(jnp.float32).T.astype(jnp.bfloat16)

    send_at = {}
    for g in range(1, levels):
        for h in range(g + 1):
            phase = 2 * g - 2 if h == g else 2 * g - 3 if h == g - 1 else 2 * g - 4
            send_at.setdefault(max(0, phase), []).append((g, h))

    flat_copy.wait()
    turn(0)
    for r in range(per_level):
        load(0, 0, r).wait()
    pl.semaphore_wait(barrier, n_prow - 1 + n_pcol - 1 + (n_prow - 1) * per_level)
    for p in range(phases):
        if p == 0:
            issue(1, 0)
            first_phase()
        else:
            for ch in range(CHUNKS):
                products(p, ch, reduce(p - 1, ch))
        for g, h in send_at.get(p, []):
            if (g, h) != (1, 0):
                issue(g, h)
        if p == 0:
            for g in range(1, levels):
                turn(g)
        else:
            finish(p - 1)
        g = (p + 2) // 2
        if p % 2 == 0 and g < levels:
            for h in range(g):
                relay(g, h)
            for h in range(g):
                collect(g, h)
                if h < g - 1:
                    later(g, h)
            if p > 0:
                write(p // 2 - 1)
        elif p % 2 == 1:
            relay(g, g)
            collect(g, g)
    finish(phases - 1)
    for g in range(1, levels):
        for h in range(g + 1):
            settle(g, h)
    if levels > 1:
        write(levels - 2)
    for ch in range(CHUNKS):
        reduce(phases - 1, ch)
    write(levels - 1)


def local(n_prow, n_pcol, factor, right_side, node_blocks, front_mask):
    levels, _, size, width = right_side.shape
    per_level = n_pcol // n_prow
    rows = width // n_prow // CHUNKS
    phases = 2 * levels - 1
    count = levels * (levels + 1) // 2
    relays = max(1, n_prow // 2 - 1)
    anywhere = pl.BlockSpec(memory_space=pl.ANY)
    smem = pl.BlockSpec(memory_space=pltpu.SMEM)
    dma = pltpu.SemaphoreType.DMA
    bf16 = jnp.bfloat16
    return pl.pallas_call(
        functools.partial(kernel, n_prow, n_pcol),
        out_shape=jax.ShapeDtypeStruct(right_side.shape, bf16),
        in_specs=[anywhere, anywhere, smem, smem],
        out_specs=pl.BlockSpec(memory_space=pltpu.VMEM),
        scratch_shapes=[
            pltpu.VMEM((count, n_pcol, size, size), bf16),
            pltpu.VMEM((levels, size, width), bf16),
            pltpu.VMEM((levels, width, size), bf16),
            pltpu.VMEM((levels, CHUNKS, n_pcol, rows, size), jnp.float32),
            pltpu.VMEM((per_level, n_prow, CHUNKS, rows, size), bf16),
            pltpu.VMEM((2, CHUNKS, n_pcol, rows, size), bf16),
            pltpu.VMEM((phases, CHUNKS, n_pcol, rows, size), bf16),
            pltpu.VMEM((levels, n_prow, CHUNKS, rows, size), bf16),
            dma((count, per_level)),
            dma,
            dma((count, per_level, n_prow // 2)),
            dma((count, per_level, relays)),
            dma((count, n_pcol)),
            dma((per_level, n_prow, CHUNKS)),
            dma((2, CHUNKS, n_pcol)),
            dma((phases, CHUNKS, n_pcol)),
            dma((levels, CHUNKS, n_prow)),
            dma((levels, CHUNKS, n_prow)),
        ],
        compiler_params=pltpu.CompilerParams(
            collective_id=0, has_side_effects=True, vmem_limit_bytes=60 * 2**20
        ),
    )(factor, right_side, node_blocks, front_mask)


def solution(mesh):
    in_specs = (P(None, "prow", None, "pcol", None, None), P(None, "pcol", None, None), P(), P())
    out_specs = P(None, "pcol", None, None)
    return jax.shard_map(
        functools.partial(local, mesh.shape["prow"], mesh.shape["pcol"]),
        mesh=mesh, in_specs=in_specs, out_specs=out_specs, check_vma=False,
    )
```

```python
import functools

import jax
import jax.numpy as jnp
from jax import lax
from jax.experimental import pallas as pl
from jax.experimental.pallas import tpu as pltpu
from jax.sharding import PartitionSpec as P

MESH = pl.DeviceIdType.MESH
CHUNKS = 2
BATCH = 4


def pair(g, h):
    return g * (g + 1) // 2 + h


def dot_nt(a, b):
    return lax.dot_general(a, b, (((1,), (1,)), ((), ())), preferred_element_type=jnp.float32)


def kernel(
    n_prow, n_pcol, factor, right, nodes, front, out,
    tiles, flat, turned, acc, first, parts, inbox, solved,
    load_sem, flat_sem, tile_send, relay_send, tile_recv,
    first_send, part_send, part_recv, share_send, share_recv,
):
    levels, _, size, width = right.shape
    per_level = n_pcol // n_prow
    rows = width // n_prow // CHUNKS
    pairs = n_prow // 2 - 1
    phases = 2 * levels - 1
    pr = lax.axis_index("prow")
    pc = lax.axis_index("pcol")
    near = pr + 1 - 2 * lax.rem(pr, 2)

    def device(row, col):
        return {"prow": row, "pcol": col}

    def remote(src, dst, send, recv, row, col):
        return pltpu.make_async_remote_copy(
            src_ref=src, dst_ref=dst, send_sem=send, recv_sem=recv,
            device_id=device(row, col), device_id_type=MESH,
        )

    def arrived(slot, sem):
        remote(slot, slot, share_send.at[0, 0, 0], sem, pr, pc).wait_recv()

    barrier = pltpu.get_barrier_semaphore()
    home = lax.rem(pc, n_prow)

    def greet(row, col):
        pl.semaphore_signal(barrier, inc=1, device_id=device(row, col), device_id_type=MESH)

    for k in range(1, n_prow):
        greet(lax.rem(pr + k, n_prow), pc)
    for k in range(1, n_pcol):
        greet(pr, lax.rem(pc + k, n_pcol))

    @pl.when(home != pr)
    def _():
        for k in range(n_pcol):
            greet(home, lax.rem(pc + k, n_pcol))

    def place(r):
        return r * n_prow + pr

    def load(g, h, r):
        return pltpu.make_async_copy(
            factor.at[per_level * g + r, 0, h, 0], tiles.at[pair(g, h), place(r)],
            load_sem.at[pair(g, h), r],
        )

    flat_copy = pltpu.make_async_copy(right.at[:, 0], flat, flat_sem)
    flat_copy.start()
    for g in range(levels):
        for h in range(g + 1):
            for r in range(per_level):
                load(g, h, r).start()

    ends = []
    for g in range(levels):
        base = 2 ** (levels - 1 - g) - 1
        total, ends_now = jnp.int32(0), []
        for k in range(base + 1):
            total = total + nodes[base + k]
            ends_now.append(total)
        ends.append(ends_now)

    def node(g, i):
        found = jnp.int32(2 ** (levels - 1 - g) - 1)
        for end in ends[g][:-1]:
            found = found + jnp.where(i >= end, 1, 0)
        return found

    col_node = [node(g, pc) for g in range(levels)]

    def diag_bit(g, i):
        return jnp.where((node(g, i) == col_node[g]) & (i >= pc), 1.0, 0.0).astype(jnp.float32)

    def front_bit(g, h, i):
        return front[col_node[h], g * n_pcol + i].astype(jnp.float32)

    def live(g, h, i, action):
        if g == h:
            pl.when(i >= pc)(action)
        else:
            action()

    def tile_copies(g, h, r):
        q, i = pair(g, h), place(r)
        targets = [lax.rem(pr + 2 * k, n_prow) for k in range(1, pairs + 1)] + [near]
        return [
            remote(factor.at[per_level * g + r, 0, h, 0], tiles.at[q, i],
                   tile_send.at[q, r, k], tile_recv.at[q, i], target, pc)
            for k, target in enumerate(targets)
        ]

    def relay_copies(g, h, r):
        q = pair(g, h)
        copies = []
        for k in range(1, pairs + 1):
            i = r * n_prow + lax.rem(pr + 2 * k, n_prow)
            copies.append((i, remote(tiles.at[q, i], tiles.at[q, i], relay_send.at[q, r, k - 1],
                                     tile_recv.at[q, i], near, pc)))
        return copies

    def issue(g, h):
        for r in range(per_level):
            def go(r=r):
                for copy in tile_copies(g, h, r):
                    copy.start()
            live(g, h, place(r), go)

    def relay(g, h):
        for r in range(per_level):
            for i, copy in relay_copies(g, h, r):
                def go(i=i, copy=copy):
                    arrived(tiles.at[pair(g, h), i], tile_recv.at[pair(g, h), i])
                    copy.start()
                live(g, h, i, go)

    def collect(g, h):
        q = pair(g, h)
        for r in range(per_level):
            load(g, h, r).wait()
            for k in range(pairs + 1):
                i = r * n_prow + lax.rem(near + 2 * k, n_prow)
                live(g, h, i, lambda i=i: arrived(tiles.at[q, i], tile_recv.at[q, i]))

    def settle(g, h):
        for r in range(per_level):
            def go(r=r):
                for copy in tile_copies(g, h, r):
                    copy.wait_send()
            live(g, h, place(r), go)
            for i, copy in relay_copies(g, h, r):
                live(g, h, i, copy.wait_send)

    def first_copies(r, ch):
        return [
            remote(first.at[r, s, ch], inbox.at[0, ch, pc], first_send.at[r, s, ch],
                   part_recv.at[0, ch, pc], s, place(r))
            for s in [lax.rem(pr + k, n_prow) for k in range(n_prow)]
        ]

    def first_each(r, ch, action, stay):
        for k, copy in enumerate(first_copies(r, ch)):
            if k == 0:
                pl.when(place(r) != pc)(lambda: action(copy))
                if stay is not None:
                    pl.when(place(r) == pc)(stay)
            else:
                action(copy)

    far = [lax.rem(pc // n_prow + 1 + k, per_level) for k in range(per_level)]

    def first_phase():
        for r in far:
            i = place(r)
            value = dot_nt(turned[0], tiles[0, i]) * diag_bit(0, i)
            first[r] = value.astype(jnp.bfloat16).reshape(n_prow, CHUNKS, rows, size)

            @pl.when(i >= pc)
            def _():
                for ch in range(CHUNKS):
                    def stay(ch=ch):
                        inbox[0, ch, pc] = first[r, pr, ch]
                    first_each(r, ch, lambda copy: copy.start(), stay)

    def first_settle():
        for r in far:
            @pl.when(place(r) >= pc)
            def _():
                for ch in range(CHUNKS):
                    first_each(r, ch, lambda copy: copy.wait_send(), None)

    def part_copy(p, ch, i):
        return remote(parts.at[p % 2, ch, i], inbox.at[p, ch, pc], part_send.at[p % 2, ch, i],
                      part_recv.at[p, ch, pc], pr, i)

    def each_group(body):
        def group(k):
            return [lax.rem(pc + n_pcol // 2 + k * BATCH + m, n_pcol) for m in range(BATCH)]

        if n_pcol <= 8:
            for k in range(n_pcol // BATCH):
                body(group(k))
        else:
            def loop(k, carry):
                body(group(k))
                return carry

            lax.fori_loop(0, n_pcol // BATCH, loop, 0)

    def goes(g, h, i):
        return (i != pc) & (i >= pc) if g == h else i != pc

    def products(p, ch, x):
        g = (p + 1) // 2
        h = g if p % 2 == 0 else g - 1

        def result(i):
            value = dot_nt(x, tiles[pair(g, h), i])
            if p % 2 == 0:
                return value * diag_bit(g, i)
            value = value * front_bit(g, h, i)
            return value + acc[g, i, pl.ds(ch * rows, rows)] if g > 1 else value

        def body(group):
            values = [result(i).astype(jnp.bfloat16) for i in group]
            for i, value in zip(group, values):
                parts[p % 2, ch, i] = value
            for i in group:
                pl.when(goes(g, h, i))(part_copy(p, ch, i).start)

        each_group(body)
        inbox[p, ch, pc] = parts[p % 2, ch, pc]

    def finish(p):
        if p == 0:
            return first_settle()
        g = (p + 1) // 2
        h = g if p % 2 == 0 else g - 1
        for ch in range(CHUNKS):
            def body(group):
                for i in group:
                    pl.when(goes(g, h, i))(part_copy(p, ch, i).wait_send)
            each_group(body)

    def later(g, h):
        x = solved[h, pr].reshape(CHUNKS * rows, size)

        def body(group):
            values = [dot_nt(x, tiles[pair(g, h), i]) * front_bit(g, h, i) for i in group]
            for i, value in zip(group, values):
                acc[g, i] = value if h == 0 else acc[g, i] + value

        each_group(body)

    def share_copies(g, ch):
        return [
            remote(solved.at[g, pr, ch], solved.at[g, pr, ch], share_send.at[g, ch, s],
                   share_recv.at[g, ch, pr], s, pc)
            for s in [lax.rem(pr + k, n_prow) for k in range(1, n_prow)]
        ]

    def reduce(p, ch):
        def add(source, total):
            own = source == pc
            if p == 0:
                own = own & (home == pr)
            pl.when(jnp.logical_not(own))(
                lambda: arrived(inbox.at[p, ch, source], part_recv.at[p, ch, source])
            )
            return total + inbox[p, ch, source].astype(jnp.float32)

        total = jnp.zeros((rows, size), jnp.float32)
        g = (p + 1) // 2
        if p % 2 == 0:
            x = lax.fori_loop(0, pc + 1, add, total).astype(jnp.bfloat16)
            solved[g, pr, ch] = x
            for copy in share_copies(g, ch):
                copy.start()
            return x
        total = lax.fori_loop(0, n_pcol, add, total)
        start = pl.multiple_of((pr * CHUNKS + ch) * rows, rows)
        return (turned[g, pl.ds(start, rows), :].astype(jnp.float32) - total).astype(jnp.bfloat16)

    def write(g):
        for ch in range(CHUNKS):
            for k in range(1, n_prow):
                s = lax.rem(pr + k, n_prow)
                arrived(solved.at[g, s, ch], share_recv.at[g, ch, s])
        out[g, 0] = solved[g].reshape(width, size).astype(jnp.float32).T.astype(jnp.bfloat16)
        for ch in range(CHUNKS):
            for copy in share_copies(g, ch):
                copy.wait_send()

    def turn(g):
        turned[g] = flat[g].astype(jnp.float32).T.astype(jnp.bfloat16)

    send_at = {}
    for g in range(1, levels):
        for h in range(g + 1):
            phase = 2 * g - 2 if h == g else 2 * g - 3 if h == g - 1 else 2 * g - 4
            send_at.setdefault(max(0, phase), []).append((g, h))

    flat_copy.wait()
    turn(0)
    for r in range(per_level):
        load(0, 0, r).wait()
    pl.semaphore_wait(barrier, n_prow - 1 + n_pcol - 1 + (n_prow - 1) * per_level)
    for p in range(phases):
        if p == 0:
            issue(1, 0)
            first_phase()
        else:
            for ch in range(CHUNKS):
                products(p, ch, reduce(p - 1, ch))
        for g, h in send_at.get(p, []):
            if (g, h) != (1, 0):
                issue(g, h)
        if p == 0:
            for g in range(1, levels):
                turn(g)
        else:
            finish(p - 1)
        g = (p + 2) // 2
        if p % 2 == 0 and g < levels:
            relay(g, g - 1)
            collect(g, g - 1)
            if g > 1:
                relay(g, g - 2)
                collect(g, g - 2)
                later(g, g - 2)
                write(g - 2)
        elif p % 2 == 1:
            relay(g, g)
            collect(g, g)
            for h in range(g - 1 if g + 1 < levels else 0):
                relay(g + 1, h)
                collect(g + 1, h)
                later(g + 1, h)
    finish(phases - 1)
    for g in range(1, levels):
        for h in range(g + 1):
            settle(g, h)
    if levels > 1:
        write(levels - 2)
    for ch in range(CHUNKS):
        reduce(phases - 1, ch)
    write(levels - 1)


def local(n_prow, n_pcol, factor, right_side, node_blocks, front_mask):
    levels, _, size, width = right_side.shape
    per_level = n_pcol // n_prow
    rows = width // n_prow // CHUNKS
    phases = 2 * levels - 1
    count = levels * (levels + 1) // 2
    relays = max(1, n_prow // 2 - 1)
    anywhere = pl.BlockSpec(memory_space=pl.ANY)
    smem = pl.BlockSpec(memory_space=pltpu.SMEM)
    dma = pltpu.SemaphoreType.DMA
    bf16 = jnp.bfloat16
    return pl.pallas_call(
        functools.partial(kernel, n_prow, n_pcol),
        out_shape=jax.ShapeDtypeStruct(right_side.shape, bf16),
        in_specs=[anywhere, anywhere, smem, smem],
        out_specs=pl.BlockSpec(memory_space=pltpu.VMEM),
        scratch_shapes=[
            pltpu.VMEM((count, n_pcol, size, size), bf16),
            pltpu.VMEM((levels, size, width), bf16),
            pltpu.VMEM((levels, width, size), bf16),
            pltpu.VMEM((levels, n_pcol, CHUNKS * rows, size), jnp.float32),
            pltpu.VMEM((per_level, n_prow, CHUNKS, rows, size), bf16),
            pltpu.VMEM((2, CHUNKS, n_pcol, rows, size), bf16),
            pltpu.VMEM((phases, CHUNKS, n_pcol, rows, size), bf16),
            pltpu.VMEM((levels, n_prow, CHUNKS, rows, size), bf16),
            dma((count, per_level)),
            dma,
            dma((count, per_level, n_prow // 2)),
            dma((count, per_level, relays)),
            dma((count, n_pcol)),
            dma((per_level, n_prow, CHUNKS)),
            dma((2, CHUNKS, n_pcol)),
            dma((phases, CHUNKS, n_pcol)),
            dma((levels, CHUNKS, n_prow)),
            dma((levels, CHUNKS, n_prow)),
        ],
        compiler_params=pltpu.CompilerParams(
            collective_id=0, has_side_effects=True, vmem_limit_bytes=60 * 2**20
        ),
    )(factor, right_side, node_blocks, front_mask)


def solution(mesh):
    in_specs = (P(None, "prow", None, "pcol", None, None), P(None, "pcol", None, None), P(), P())
    out_specs = P(None, "pcol", None, None)
    return jax.shard_map(
        functools.partial(local, mesh.shape["prow"], mesh.shape["pcol"]),
        mesh=mesh, in_specs=in_specs, out_specs=out_specs, check_vma=False,
    )
```

```python
import functools

import jax
import jax.numpy as jnp
from jax import lax
from jax.experimental import pallas as pl
from jax.experimental.pallas import tpu as pltpu
from jax.sharding import PartitionSpec as P

MESH = pl.DeviceIdType.MESH
CHUNKS = 2
BATCH = 4


def pair(g, h):
    return g * (g + 1) // 2 + h


def dot_nt(a, b):
    return lax.dot_general(a, b, (((1,), (1,)), ((), ())), preferred_element_type=jnp.float32)


def kernel(
    n_prow, n_pcol, factor, right, nodes, front, out,
    own, tiles, flat, turned, acc, first, parts, inbox, mates, solved,
    load_sem, flat_sem, tile_send, relay_send, tile_recv,
    first_send, part_send, part_recv, mate_send, mate_recv, share_send, share_recv,
):
    levels, _, size, width = right.shape
    per_level = n_pcol // n_prow
    rows = width // n_prow // CHUNKS
    pairs = n_prow // 2 - 1
    phases = 2 * levels - 1
    pr = lax.axis_index("prow")
    pc = lax.axis_index("pcol")
    near = pr + 1 - 2 * lax.rem(pr, 2)
    half = n_pcol // 2
    side = pc // half
    mate = pc + 1 - 2 * lax.rem(pc, 2)
    adds = lax.rem(pc, 2) == lax.rem(pr, 2)

    def device(row, col):
        return {"prow": row, "pcol": col}

    def remote(src, dst, send, recv, row, col):
        return pltpu.make_async_remote_copy(
            src_ref=src, dst_ref=dst, send_sem=send, recv_sem=recv,
            device_id=device(row, col), device_id_type=MESH,
        )

    def arrived(slot, sem):
        remote(slot, slot, share_send.at[0, 0, 0], sem, pr, pc).wait_recv()

    barrier = pltpu.get_barrier_semaphore()
    home = lax.rem(pc, n_prow)

    def greet(row, col):
        pl.semaphore_signal(barrier, inc=1, device_id=device(row, col), device_id_type=MESH)

    for k in range(1, n_prow):
        greet(lax.rem(pr + k, n_prow), pc)
    for k in range(1, n_pcol):
        greet(pr, lax.rem(pc + k, n_pcol))

    @pl.when(home != pr)
    def _():
        for k in range(n_pcol):
            greet(home, lax.rem(pc + k, n_pcol))

    def place(r):
        return r * n_prow + pr

    def load(g, h, r):
        return pltpu.make_async_copy(
            factor.at[per_level * g + r, 0, h, 0],
            tiles.at[g, place(r)] if g == h else own.at[pair(g, h), r],
            load_sem.at[pair(g, h), r],
        )

    flat_copy = pltpu.make_async_copy(right.at[:, 0], flat, flat_sem)
    flat_copy.start()
    for g in range(levels):
        for h in range(g + 1):
            for r in range(per_level):
                load(g, h, r).start()

    ends = []
    for g in range(levels):
        base = 2 ** (levels - 1 - g) - 1
        total, ends_now = jnp.int32(0), []
        for k in range(base + 1):
            total = total + nodes[base + k]
            ends_now.append(total)
        ends.append(ends_now)

    def node(g, i):
        found = jnp.int32(2 ** (levels - 1 - g) - 1)
        for end in ends[g][:-1]:
            found = found + jnp.where(i >= end, 1, 0)
        return found

    col_node = [node(g, pc) for g in range(levels)]

    def diag_bit(g, i):
        return jnp.where((node(g, i) == col_node[g]) & (i >= pc), 1.0, 0.0).astype(jnp.float32)

    def front_bit(g, h, i):
        return front[col_node[h], g * n_pcol + i].astype(jnp.float32)

    def live(i, action):
        pl.when(i >= pc)(action)

    def tile_copies(g, r):
        i = place(r)
        targets = [lax.rem(pr + 2 * k, n_prow) for k in range(1, pairs + 1)] + [near]
        return [
            remote(factor.at[per_level * g + r, 0, g, 0], tiles.at[g, i],
                   tile_send.at[g, r, k], tile_recv.at[g, i], target, pc)
            for k, target in enumerate(targets)
        ]

    def relay_copies(g, r):
        copies = []
        for k in range(1, pairs + 1):
            i = r * n_prow + lax.rem(pr + 2 * k, n_prow)
            copies.append((i, remote(tiles.at[g, i], tiles.at[g, i], relay_send.at[g, r, k - 1],
                                     tile_recv.at[g, i], near, pc)))
        return copies

    def issue(g):
        for r in range(per_level):
            def go(r=r):
                for copy in tile_copies(g, r):
                    copy.start()
            live(place(r), go)

    def relay(g):
        for r in range(per_level):
            for i, copy in relay_copies(g, r):
                def go(i=i, copy=copy):
                    arrived(tiles.at[g, i], tile_recv.at[g, i])
                    copy.start()
                live(i, go)

    def collect(g):
        for r in range(per_level):
            load(g, g, r).wait()
            for k in range(pairs + 1):
                i = r * n_prow + lax.rem(near + 2 * k, n_prow)
                live(i, lambda i=i: arrived(tiles.at[g, i], tile_recv.at[g, i]))

    def settle(g):
        for r in range(per_level):
            def go(r=r):
                for copy in tile_copies(g, r):
                    copy.wait_send()
            live(place(r), go)
            for i, copy in relay_copies(g, r):
                live(i, copy.wait_send)

    few = per_level // 2

    def far_row(m):
        return (1 - side) * few + m

    def near_row(m):
        return side * few + m

    def row_sends(p, ch, r, keep):
        copies = []
        for k in range(n_prow):
            s = lax.rem(pr + k, n_prow)
            copy = remote(first.at[p % 2, ch, r, s], inbox.at[p, ch, pc], first_send.at[p % 2, ch, r, s],
                          part_recv.at[p, ch, pc], s, place(r))
            copies.append((copy, (place(r) != pc) if keep and k == 0 else None))
        return copies

    def each(copies, action):
        for copy, test in copies:
            if test is None:
                action(copy)
            else:
                pl.when(test)(lambda copy=copy: action(copy))

    def row_mate(p, ch, m):
        return remote(first.at[p % 2, ch, far_row(m)], mates.at[p, ch, pl.ds(m * n_prow, n_prow)],
                      mate_send.at[p % 2, ch, m], mate_recv.at[p, ch, m], pr, mate)

    def crosses(p):
        return side == 0 if p % 2 == 0 else side >= 0

    def row_products(p, ch):
        g = (p + 1) // 2
        if p == 0:
            x = turned[0].reshape(n_prow, CHUNKS, rows, size)[:, ch]
        else:
            gather(g - 1, ch)
            x = solved[g - 1, :, ch]
        x = x.reshape(n_prow * rows, size)
        for r in [far_row(m) for m in range(few)] + [near_row(m) for m in range(few)]:
            if p == 0:
                value = dot_nt(x, tiles[0, place(r)]) * diag_bit(0, place(r))
            else:
                value = dot_nt(x, own[pair(g, g - 1), r]) * front_bit(g, g - 1, place(r))
            value = value.reshape(n_prow, rows, size)
            if g > 1:
                value = value + acc[g, r, :, ch]
            first[p % 2, ch, r] = value.astype(jnp.bfloat16)
        for m in range(few):
            pl.when(crosses(p) & jnp.logical_not(adds))(row_mate(p, ch, m).start)
        for m in range(few):
            r = near_row(m)

            def go(r=r):
                each(row_sends(p, ch, r, True), lambda copy: copy.start())

                @pl.when(place(r) == pc)
                def _():
                    inbox[p, ch, pc] = first[p % 2, ch, r, pr]
            if p == 0:
                live(place(r), go)
            else:
                go()

    def row_combine(p, ch):
        @pl.when(crosses(p) & adds)
        def _():
            for m in range(few):
                r = far_row(m)
                slot = mates.at[p, ch, pl.ds(m * n_prow, n_prow)]
                arrived(slot, mate_recv.at[p, ch, m])
                total = first[p % 2, ch, r].astype(jnp.float32) + slot[...].astype(jnp.float32)
                first[p % 2, ch, r] = total.astype(jnp.bfloat16)
                each(row_sends(p, ch, r, False), lambda copy: copy.start())

    def row_finish(p, ch):
        for m in range(few):
            r = near_row(m)

            def go(r=r):
                each(row_sends(p, ch, r, True), lambda copy: copy.wait_send())
            if p == 0:
                live(place(r), go)
            else:
                go()
            pl.when(crosses(p) & jnp.logical_not(adds))(row_mate(p, ch, m).wait_send)

            @pl.when(crosses(p) & adds)
            def _():
                each(row_sends(p, ch, far_row(m), False), lambda copy: copy.wait_send())

    def part_copy(p, ch, i):
        return remote(parts.at[p // 2 % 2, ch, i], inbox.at[p, ch, pc], part_send.at[p // 2 % 2, ch, i],
                      part_recv.at[p, ch, pc], pr, i)

    def part_mate(p, ch, m):
        return remote(parts.at[p // 2 % 2, ch, half + 2 * m + lax.rem(mate, 2)], mates.at[p, ch, m],
                      mate_send.at[p % 2, ch, m], mate_recv.at[p, ch, m], pr, mate)

    def column_products(p, ch, x):
        g = p // 2

        def batch(base):
            for i in [base + m for m in range(BATCH)]:
                value = dot_nt(x, tiles[g, i]) * diag_bit(g, i)
                parts[p // 2 % 2, ch, i] = value.astype(jnp.bfloat16)

        if n_pcol <= 8:
            for k in range(n_pcol // BATCH - 1, -1, -1):
                batch(k * BATCH)
        else:
            def loop(k, carry):
                batch(k * BATCH)
                return carry

            lax.fori_loop(0, n_pcol // BATCH, loop, 0)

        @pl.when(side == 0)
        def _():
            for m in range(half // 2):
                part_mate(p, ch, m).start()

        for m in range(half):
            i = side * half + m
            pl.when(i > pc)(part_copy(p, ch, i).start)
        inbox[p, ch, pc] = parts[p // 2 % 2, ch, pc]

    def column_combine(p, ch):
        @pl.when(side == 0)
        def _():
            for m in range(half // 2):
                i = half + 2 * m + lax.rem(pc, 2)
                arrived(mates.at[p, ch, m], mate_recv.at[p, ch, m])
                total = parts[p // 2 % 2, ch, i].astype(jnp.float32) + mates[p, ch, m].astype(jnp.float32)
                parts[p // 2 % 2, ch, i] = total.astype(jnp.bfloat16)
                part_copy(p, ch, i).start()

    def column_finish(p, ch):
        @pl.when(side == 0)
        def _():
            for m in range(half // 2):
                part_mate(p, ch, m).wait_send()
                part_copy(p, ch, half + 2 * m + lax.rem(pc, 2)).wait_send()

        for m in range(half):
            i = side * half + m
            pl.when(i > pc)(part_copy(p, ch, i).wait_send)

    def by_rows(p):
        return p == 0 or p % 2 == 1

    def finish(p):
        for ch in range(CHUNKS):
            (row_finish if by_rows(p) else column_finish)(p, ch)

    def later(g, h):
        x = solved[h].reshape(width, size)
        for r in range(per_level):
            load(g, h, r).wait()
            value = dot_nt(x, own[pair(g, h), r]) * front_bit(g, h, place(r))
            value = value.reshape(n_prow, CHUNKS, rows, size)
            acc[g, r] = value if h == 0 else acc[g, r] + value

    def share_copies(g, ch):
        return [
            remote(solved.at[g, pr, ch], solved.at[g, pr, ch], share_send.at[g, ch, s],
                   share_recv.at[g, ch, pr], s, pc)
            for s in [lax.rem(pr + k, n_prow) for k in range(1, n_prow)]
        ]

    def reduce(p, ch):
        def add(source, total):
            kept = source == pc
            if by_rows(p):
                kept = kept & (home == pr)
            pl.when(jnp.logical_not(kept))(
                lambda: arrived(inbox.at[p, ch, source], part_recv.at[p, ch, source])
            )
            return total + inbox[p, ch, source].astype(jnp.float32)

        total = jnp.zeros((rows, size), jnp.float32)
        near_count = lax.rem(pc, half) + 1 if p % 2 == 0 else half
        far_count = side * (half // 2) if p % 2 == 0 else half // 2
        total = lax.fori_loop(0, near_count, lambda m, t: add(side * half + m, t), total)
        total = lax.fori_loop(
            0, far_count, lambda m, t: add((1 - side) * half + 2 * m + lax.rem(pc, 2), t), total
        )
        g = (p + 1) // 2
        if p % 2 == 0:
            solved[g, pr, ch] = total.astype(jnp.bfloat16)
            for copy in share_copies(g, ch):
                copy.start()
            return None
        start = pl.multiple_of((pr * CHUNKS + ch) * rows, rows)
        return (turned[g, pl.ds(start, rows), :].astype(jnp.float32) - total).astype(jnp.bfloat16)

    def gather(g, ch):
        for k in range(1, n_prow):
            s = lax.rem(pr + k, n_prow)
            arrived(solved.at[g, s, ch], share_recv.at[g, ch, s])

    def write(g):
        out[g, 0] = solved[g].reshape(width, size).astype(jnp.float32).T.astype(jnp.bfloat16)
        for ch in range(CHUNKS):
            for copy in share_copies(g, ch):
                copy.wait_send()

    def turn(g):
        turned[g] = flat[g].astype(jnp.float32).T.astype(jnp.bfloat16)

    flat_copy.wait()
    turn(0)
    for r in range(per_level):
        load(0, 0, r).wait()
    pl.semaphore_wait(barrier, n_prow - 1 + n_pcol - 1 + (n_prow - 1) * per_level)
    for p in range(phases):
        g = (p + 1) // 2
        if p % 2 == 1:
            for r in range(per_level):
                load(g, g - 1, r).wait()
        if p > 0 and p % 2 == 0:
            collect(g)
        if p % 2 == 1:
            for ch in range(CHUNKS):
                reduce(p - 1, ch)
        for ch in range(CHUNKS):
            if by_rows(p):
                row_products(p, ch)
            else:
                column_products(p, ch, reduce(p - 1, ch))
        for ch in range(CHUNKS):
            (row_combine if by_rows(p) else column_combine)(p, ch)
        if p == 0:
            issue(1)
            for level in range(1, levels):
                turn(level)
        else:
            finish(p - 1)
        if p % 2 == 1:
            if g + 1 < levels:
                issue(g + 1)
            relay(g)
            if g > 1 and g + 1 < levels:
                for h in range(g - 1):
                    later(g + 1, h)
            write(g - 1)
        elif 0 < g < levels - 1:
            later(g + 1, g - 1)
    finish(phases - 1)
    for g in range(1, levels):
        settle(g)
    for ch in range(CHUNKS):
        reduce(phases - 1, ch)
    for ch in range(CHUNKS):
        gather(levels - 1, ch)
    write(levels - 1)


def local(n_prow, n_pcol, factor, right_side, node_blocks, front_mask):
    levels, _, size, width = right_side.shape
    per_level = n_pcol // n_prow
    rows = width // n_prow // CHUNKS
    phases = 2 * levels - 1
    count = levels * (levels + 1) // 2
    relays = max(1, n_prow // 2 - 1)
    anywhere = pl.BlockSpec(memory_space=pl.ANY)
    smem = pl.BlockSpec(memory_space=pltpu.SMEM)
    dma = pltpu.SemaphoreType.DMA
    bf16 = jnp.bfloat16
    return pl.pallas_call(
        functools.partial(kernel, n_prow, n_pcol),
        out_shape=jax.ShapeDtypeStruct(right_side.shape, bf16),
        in_specs=[anywhere, anywhere, smem, smem],
        out_specs=pl.BlockSpec(memory_space=pltpu.VMEM),
        scratch_shapes=[
            pltpu.VMEM((count, per_level, size, size), bf16),
            pltpu.VMEM((levels, n_pcol, size, size), bf16),
            pltpu.VMEM((levels, size, width), bf16),
            pltpu.VMEM((levels, width, size), bf16),
            pltpu.VMEM((levels, per_level, n_prow, CHUNKS, rows, size), jnp.float32),
            pltpu.VMEM((2, CHUNKS, per_level, n_prow, rows, size), bf16),
            pltpu.VMEM((2, CHUNKS, n_pcol, rows, size), bf16),
            pltpu.VMEM((phases, CHUNKS, n_pcol, rows, size), bf16),
            pltpu.VMEM((phases, CHUNKS, n_pcol // 2, rows, size), bf16),
            pltpu.VMEM((levels, n_prow, CHUNKS, rows, size), bf16),
            dma((count, per_level)),
            dma,
            dma((levels, per_level, n_prow // 2)),
            dma((levels, per_level, relays)),
            dma((levels, n_pcol)),
            dma((2, CHUNKS, per_level, n_prow)),
            dma((2, CHUNKS, n_pcol)),
            dma((phases, CHUNKS, n_pcol)),
            dma((2, CHUNKS, n_pcol // 2)),
            dma((phases, CHUNKS, n_pcol // 2)),
            dma((levels, CHUNKS, n_prow)),
            dma((levels, CHUNKS, n_prow)),
        ],
        compiler_params=pltpu.CompilerParams(
            collective_id=0, has_side_effects=True, vmem_limit_bytes=60 * 2**20
        ),
    )(factor, right_side, node_blocks, front_mask)


def solution(mesh):
    in_specs = (P(None, "prow", None, "pcol", None, None), P(None, "pcol", None, None), P(), P())
    out_specs = P(None, "pcol", None, None)
    return jax.shard_map(
        functools.partial(local, mesh.shape["prow"], mesh.shape["pcol"]),
        mesh=mesh, in_specs=in_specs, out_specs=out_specs, check_vma=False,
    )
```

```python
import functools

import jax
import jax.numpy as jnp
from jax import lax
from jax.experimental import pallas as pl
from jax.experimental.pallas import tpu as pltpu
from jax.sharding import PartitionSpec as P

MESH = pl.DeviceIdType.MESH
CHUNKS = 1
BATCH = 4


def pair(g, h):
    return g * (g + 1) // 2 + h


def dot_nt(a, b):
    return lax.dot_general(a, b, (((1,), (1,)), ((), ())), preferred_element_type=jnp.float32)


def kernel(
    n_prow, n_pcol, factor, right, nodes, front, out,
    own, tiles, flat, turned, acc, first, parts, inbox, mates, solved,
    load_sem, flat_sem, tile_send, relay_send, tile_recv,
    first_send, part_send, part_recv, mate_send, mate_recv, share_send, share_recv,
):
    levels, _, size, width = right.shape
    per_level = n_pcol // n_prow
    rows = width // n_prow // CHUNKS
    pairs = n_prow // 2 - 1
    phases = 2 * levels - 1
    pr = lax.axis_index("prow")
    pc = lax.axis_index("pcol")
    near = pr + 1 - 2 * lax.rem(pr, 2)
    half = n_pcol // 2
    side = pc // half
    mate = pc + 1 - 2 * lax.rem(pc, 2)
    adds = lax.rem(pc, 2) == lax.rem(pr, 2)

    def device(row, col):
        return {"prow": row, "pcol": col}

    def remote(src, dst, send, recv, row, col):
        return pltpu.make_async_remote_copy(
            src_ref=src, dst_ref=dst, send_sem=send, recv_sem=recv,
            device_id=device(row, col), device_id_type=MESH,
        )

    def arrived(slot, sem):
        remote(slot, slot, share_send.at[0, 0, 0], sem, pr, pc).wait_recv()

    barrier = pltpu.get_barrier_semaphore()
    home = lax.rem(pc, n_prow)

    def greet(row, col):
        pl.semaphore_signal(barrier, inc=1, device_id=device(row, col), device_id_type=MESH)

    for k in range(1, n_prow):
        greet(lax.rem(pr + k, n_prow), pc)
    for k in range(1, n_pcol):
        greet(pr, lax.rem(pc + k, n_pcol))

    @pl.when(home != pr)
    def _():
        for k in range(n_pcol):
            greet(home, lax.rem(pc + k, n_pcol))

    def place(r):
        return r * n_prow + pr

    def load(g, h, r):
        return pltpu.make_async_copy(
            factor.at[per_level * g + r, 0, h, 0],
            tiles.at[g, place(r)] if g == h else own.at[pair(g, h), r],
            load_sem.at[pair(g, h), r],
        )

    flat_copy = pltpu.make_async_copy(right.at[:, 0], flat, flat_sem)
    flat_copy.start()
    for g in range(levels):
        for h in range(g + 1):
            for r in range(per_level):
                load(g, h, r).start()

    ends = []
    for g in range(levels):
        base = 2 ** (levels - 1 - g) - 1
        total, ends_now = jnp.int32(0), []
        for k in range(base + 1):
            total = total + nodes[base + k]
            ends_now.append(total)
        ends.append(ends_now)

    def node(g, i):
        found = jnp.int32(2 ** (levels - 1 - g) - 1)
        for end in ends[g][:-1]:
            found = found + jnp.where(i >= end, 1, 0)
        return found

    col_node = [node(g, pc) for g in range(levels)]

    def diag_bit(g, i):
        return jnp.where((node(g, i) == col_node[g]) & (i >= pc), 1.0, 0.0).astype(jnp.float32)

    def front_bit(g, h, i):
        return front[col_node[h], g * n_pcol + i].astype(jnp.float32)

    def live(i, action):
        pl.when(i >= pc)(action)

    def tile_copies(g, r):
        i = place(r)
        targets = [lax.rem(pr + 2 * k, n_prow) for k in range(1, pairs + 1)] + [near]
        return [
            remote(factor.at[per_level * g + r, 0, g, 0], tiles.at[g, i],
                   tile_send.at[g, r, k], tile_recv.at[g, i], target, pc)
            for k, target in enumerate(targets)
        ]

    def relay_copies(g, r):
        copies = []
        for k in range(1, pairs + 1):
            i = r * n_prow + lax.rem(pr + 2 * k, n_prow)
            copies.append((i, remote(tiles.at[g, i], tiles.at[g, i], relay_send.at[g, r, k - 1],
                                     tile_recv.at[g, i], near, pc)))
        return copies

    def issue(g):
        for r in range(per_level):
            def go(r=r):
                for copy in tile_copies(g, r):
                    copy.start()
            live(place(r), go)

    def relay(g):
        for r in range(per_level):
            for i, copy in relay_copies(g, r):
                def go(i=i, copy=copy):
                    arrived(tiles.at[g, i], tile_recv.at[g, i])
                    copy.start()
                live(i, go)

    def collect(g):
        for r in range(per_level):
            load(g, g, r).wait()
            for k in range(pairs + 1):
                i = r * n_prow + lax.rem(near + 2 * k, n_prow)
                live(i, lambda i=i: arrived(tiles.at[g, i], tile_recv.at[g, i]))

    def settle(g):
        for r in range(per_level):
            def go(r=r):
                for copy in tile_copies(g, r):
                    copy.wait_send()
            live(place(r), go)
            for i, copy in relay_copies(g, r):
                live(i, copy.wait_send)

    few = per_level // 2

    def far_row(m):
        return (1 - side) * few + m

    def near_row(m):
        return side * few + m

    def row_sends(p, ch, r, keep):
        copies = []
        for k in range(n_prow):
            s = lax.rem(pr + k, n_prow)
            copy = remote(first.at[p % 2, ch, r, s], inbox.at[p, ch, pc], first_send.at[p % 2, ch, r, s],
                          part_recv.at[p, ch, pc], s, place(r))
            copies.append((copy, (place(r) != pc) if keep and k == 0 else None))
        return copies

    def each(copies, action):
        for copy, test in copies:
            if test is None:
                action(copy)
            else:
                pl.when(test)(lambda copy=copy: action(copy))

    def row_mate(p, ch, m):
        return remote(first.at[p % 2, ch, far_row(m)], mates.at[p, ch, pl.ds(m * n_prow, n_prow)],
                      mate_send.at[p % 2, ch, m], mate_recv.at[p, ch, m], pr, mate)

    def crosses(p):
        return side == 0 if p % 2 == 0 else side >= 0

    def row_products(p, ch):
        g = (p + 1) // 2
        if p == 0:
            x = turned[0].reshape(n_prow, CHUNKS, rows, size)[:, ch]
        else:
            gather(g - 1, ch)
            x = solved[g - 1, :, ch]
        x = x.reshape(n_prow * rows, size)
        for r in [far_row(m) for m in range(few)] + [near_row(m) for m in range(few)]:
            if p == 0:
                value = dot_nt(x, tiles[0, place(r)]) * diag_bit(0, place(r))
            else:
                value = dot_nt(x, own[pair(g, g - 1), r]) * front_bit(g, g - 1, place(r))
            value = value.reshape(n_prow, rows, size)
            if g > 1:
                value = value + acc[g, r, :, ch]
            first[p % 2, ch, r] = value.astype(jnp.bfloat16)
        for m in range(few):
            pl.when(crosses(p) & jnp.logical_not(adds))(row_mate(p, ch, m).start)
        for m in range(few):
            r = near_row(m)

            def go(r=r):
                each(row_sends(p, ch, r, True), lambda copy: copy.start())

                @pl.when(place(r) == pc)
                def _():
                    inbox[p, ch, pc] = first[p % 2, ch, r, pr]
            if p == 0:
                live(place(r), go)
            else:
                go()

    def row_combine(p, ch):
        @pl.when(crosses(p) & adds)
        def _():
            for m in range(few):
                r = far_row(m)
                slot = mates.at[p, ch, pl.ds(m * n_prow, n_prow)]
                arrived(slot, mate_recv.at[p, ch, m])
                total = first[p % 2, ch, r].astype(jnp.float32) + slot[...].astype(jnp.float32)
                first[p % 2, ch, r] = total.astype(jnp.bfloat16)
                each(row_sends(p, ch, r, False), lambda copy: copy.start())

    def row_finish(p, ch):
        for m in range(few):
            r = near_row(m)

            def go(r=r):
                each(row_sends(p, ch, r, True), lambda copy: copy.wait_send())
            if p == 0:
                live(place(r), go)
            else:
                go()
            pl.when(crosses(p) & jnp.logical_not(adds))(row_mate(p, ch, m).wait_send)

            @pl.when(crosses(p) & adds)
            def _():
                each(row_sends(p, ch, far_row(m), False), lambda copy: copy.wait_send())

    def part_copy(p, ch, i):
        return remote(parts.at[p // 2 % 2, ch, i], inbox.at[p, ch, pc], part_send.at[p // 2 % 2, ch, i],
                      part_recv.at[p, ch, pc], pr, i)

    def part_mate(p, ch, m):
        return remote(parts.at[p // 2 % 2, ch, half + 2 * m + lax.rem(mate, 2)], mates.at[p, ch, m],
                      mate_send.at[p % 2, ch, m], mate_recv.at[p, ch, m], pr, mate)

    def column_products(p, ch, x):
        g = p // 2

        def batch(base):
            for i in [base + m for m in range(BATCH)]:
                value = dot_nt(x, tiles[g, i]) * diag_bit(g, i)
                parts[p // 2 % 2, ch, i] = value.astype(jnp.bfloat16)

        if n_pcol <= 8:
            for k in range(n_pcol // BATCH - 1, -1, -1):
                batch(k * BATCH)
        else:
            def loop(k, carry):
                batch(k * BATCH)
                return carry

            lax.fori_loop(0, n_pcol // BATCH, loop, 0)

        @pl.when(side == 0)
        def _():
            for m in range(half // 2):
                part_mate(p, ch, m).start()

        for m in range(half):
            i = side * half + m
            pl.when(i > pc)(part_copy(p, ch, i).start)
        inbox[p, ch, pc] = parts[p // 2 % 2, ch, pc]

    def column_combine(p, ch):
        @pl.when(side == 0)
        def _():
            for m in range(half // 2):
                i = half + 2 * m + lax.rem(pc, 2)
                arrived(mates.at[p, ch, m], mate_recv.at[p, ch, m])
                total = parts[p // 2 % 2, ch, i].astype(jnp.float32) + mates[p, ch, m].astype(jnp.float32)
                parts[p // 2 % 2, ch, i] = total.astype(jnp.bfloat16)
                part_copy(p, ch, i).start()

    def column_finish(p, ch):
        @pl.when(side == 0)
        def _():
            for m in range(half // 2):
                part_mate(p, ch, m).wait_send()
                part_copy(p, ch, half + 2 * m + lax.rem(pc, 2)).wait_send()

        for m in range(half):
            i = side * half + m
            pl.when(i > pc)(part_copy(p, ch, i).wait_send)

    def by_rows(p):
        return p == 0 or p % 2 == 1

    def finish(p):
        for ch in range(CHUNKS):
            (row_finish if by_rows(p) else column_finish)(p, ch)

    def later(g, h):
        x = solved[h].reshape(width, size)
        for r in range(per_level):
            load(g, h, r).wait()
            value = dot_nt(x, own[pair(g, h), r]) * front_bit(g, h, place(r))
            value = value.reshape(n_prow, CHUNKS, rows, size)
            acc[g, r] = value if h == 0 else acc[g, r] + value

    def share_copies(g, ch):
        return [
            remote(solved.at[g, pr, ch], solved.at[g, pr, ch], share_send.at[g, ch, s],
                   share_recv.at[g, ch, pr], s, pc)
            for s in [lax.rem(pr + k, n_prow) for k in range(1, n_prow)]
        ]

    def reduce(p, ch):
        def add(source, total):
            kept = source == pc
            if by_rows(p):
                kept = kept & (home == pr)
            pl.when(jnp.logical_not(kept))(
                lambda: arrived(inbox.at[p, ch, source], part_recv.at[p, ch, source])
            )
            return total + inbox[p, ch, source].astype(jnp.float32)

        total = jnp.zeros((rows, size), jnp.float32)
        near_count = lax.rem(pc, half) + 1 if p % 2 == 0 else half
        far_count = side * (half // 2) if p % 2 == 0 else half // 2
        total = lax.fori_loop(0, near_count, lambda m, t: add(side * half + m, t), total)
        total = lax.fori_loop(
            0, far_count, lambda m, t: add((1 - side) * half + 2 * m + lax.rem(pc, 2), t), total
        )
        g = (p + 1) // 2
        if p % 2 == 0:
            solved[g, pr, ch] = total.astype(jnp.bfloat16)
            for copy in share_copies(g, ch):
                copy.start()
            return None
        start = pl.multiple_of((pr * CHUNKS + ch) * rows, rows)
        return (turned[g, pl.ds(start, rows), :].astype(jnp.float32) - total).astype(jnp.bfloat16)

    def gather(g, ch):
        for k in range(1, n_prow):
            s = lax.rem(pr + k, n_prow)
            arrived(solved.at[g, s, ch], share_recv.at[g, ch, s])

    def write(g):
        out[g, 0] = solved[g].reshape(width, size).astype(jnp.float32).T.astype(jnp.bfloat16)
        for ch in range(CHUNKS):
            for copy in share_copies(g, ch):
                copy.wait_send()

    def turn(g):
        turned[g] = flat[g].astype(jnp.float32).T.astype(jnp.bfloat16)

    flat_copy.wait()
    turn(0)
    for r in range(per_level):
        load(0, 0, r).wait()
    pl.semaphore_wait(barrier, n_prow - 1 + n_pcol - 1 + (n_prow - 1) * per_level)
    for p in range(phases):
        g = (p + 1) // 2
        if p % 2 == 1:
            for r in range(per_level):
                load(g, g - 1, r).wait()
        if p > 0 and p % 2 == 0:
            collect(g)
        if p % 2 == 1:
            for ch in range(CHUNKS):
                reduce(p - 1, ch)
        for ch in range(CHUNKS):
            if by_rows(p):
                row_products(p, ch)
            else:
                column_products(p, ch, reduce(p - 1, ch))
        for ch in range(CHUNKS):
            (row_combine if by_rows(p) else column_combine)(p, ch)
        if p == 0:
            issue(1)
            for level in range(1, levels):
                turn(level)
        else:
            finish(p - 1)
        if p % 2 == 1:
            if g + 1 < levels:
                issue(g + 1)
            relay(g)
            if g > 1 and g + 1 < levels:
                for h in range(g - 1):
                    later(g + 1, h)
            write(g - 1)
        elif 0 < g < levels - 1:
            later(g + 1, g - 1)
    finish(phases - 1)
    for g in range(1, levels):
        settle(g)
    for ch in range(CHUNKS):
        reduce(phases - 1, ch)
    for ch in range(CHUNKS):
        gather(levels - 1, ch)
    write(levels - 1)


def local(n_prow, n_pcol, factor, right_side, node_blocks, front_mask):
    levels, _, size, width = right_side.shape
    per_level = n_pcol // n_prow
    rows = width // n_prow // CHUNKS
    phases = 2 * levels - 1
    count = levels * (levels + 1) // 2
    relays = max(1, n_prow // 2 - 1)
    anywhere = pl.BlockSpec(memory_space=pl.ANY)
    smem = pl.BlockSpec(memory_space=pltpu.SMEM)
    dma = pltpu.SemaphoreType.DMA
    bf16 = jnp.bfloat16
    return pl.pallas_call(
        functools.partial(kernel, n_prow, n_pcol),
        out_shape=jax.ShapeDtypeStruct(right_side.shape, bf16),
        in_specs=[anywhere, anywhere, smem, smem],
        out_specs=pl.BlockSpec(memory_space=pltpu.VMEM),
        scratch_shapes=[
            pltpu.VMEM((count, per_level, size, size), bf16),
            pltpu.VMEM((levels, n_pcol, size, size), bf16),
            pltpu.VMEM((levels, size, width), bf16),
            pltpu.VMEM((levels, width, size), bf16),
            pltpu.VMEM((levels, per_level, n_prow, CHUNKS, rows, size), jnp.float32),
            pltpu.VMEM((2, CHUNKS, per_level, n_prow, rows, size), bf16),
            pltpu.VMEM((2, CHUNKS, n_pcol, rows, size), bf16),
            pltpu.VMEM((phases, CHUNKS, n_pcol, rows, size), bf16),
            pltpu.VMEM((phases, CHUNKS, n_pcol // 2, rows, size), bf16),
            pltpu.VMEM((levels, n_prow, CHUNKS, rows, size), bf16),
            dma((count, per_level)),
            dma,
            dma((levels, per_level, n_prow // 2)),
            dma((levels, per_level, relays)),
            dma((levels, n_pcol)),
            dma((2, CHUNKS, per_level, n_prow)),
            dma((2, CHUNKS, n_pcol)),
            dma((phases, CHUNKS, n_pcol)),
            dma((2, CHUNKS, n_pcol // 2)),
            dma((phases, CHUNKS, n_pcol // 2)),
            dma((levels, CHUNKS, n_prow)),
            dma((levels, CHUNKS, n_prow)),
        ],
        compiler_params=pltpu.CompilerParams(
            collective_id=0, has_side_effects=True, vmem_limit_bytes=60 * 2**20
        ),
    )(factor, right_side, node_blocks, front_mask)


def solution(mesh):
    in_specs = (P(None, "prow", None, "pcol", None, None), P(None, "pcol", None, None), P(), P())
    out_specs = P(None, "pcol", None, None)
    return jax.shard_map(
        functools.partial(local, mesh.shape["prow"], mesh.shape["pcol"]),
        mesh=mesh, in_specs=in_specs, out_specs=out_specs, check_vma=False,
    )
```

```python
import functools

import jax
import jax.numpy as jnp
from jax import lax
from jax.experimental import pallas as pl
from jax.experimental.pallas import tpu as pltpu
from jax.sharding import PartitionSpec as P

MESH = pl.DeviceIdType.MESH
CHUNKS = 2
BATCH = 4


def pair(g, h):
    return g * (g + 1) // 2 + h


def dot_nt(a, b):
    return lax.dot_general(a, b, (((1,), (1,)), ((), ())), preferred_element_type=jnp.float32)


def kernel(
    n_prow, n_pcol, factor, right, nodes, front, out,
    own, tiles, flat, turned, acc, first, parts, inbox, solved,
    load_sem, flat_sem, tile_send, relay_send, tile_recv,
    first_send, part_send, part_recv, share_send, share_recv,
):
    levels, _, size, width = right.shape
    per_level = n_pcol // n_prow
    rows = width // n_prow // CHUNKS
    pairs = n_prow // 2 - 1
    phases = 2 * levels - 1
    pr = lax.axis_index("prow")
    pc = lax.axis_index("pcol")
    near = pr + 1 - 2 * lax.rem(pr, 2)

    def device(row, col):
        return {"prow": row, "pcol": col}

    def remote(src, dst, send, recv, row, col):
        return pltpu.make_async_remote_copy(
            src_ref=src, dst_ref=dst, send_sem=send, recv_sem=recv,
            device_id=device(row, col), device_id_type=MESH,
        )

    def arrived(slot, sem):
        remote(slot, slot, share_send.at[0, 0, 0], sem, pr, pc).wait_recv()

    barrier = pltpu.get_barrier_semaphore()
    home = lax.rem(pc, n_prow)

    def greet(row, col):
        pl.semaphore_signal(barrier, inc=1, device_id=device(row, col), device_id_type=MESH)

    for k in range(1, n_prow):
        greet(lax.rem(pr + k, n_prow), pc)
    for k in range(1, n_pcol):
        greet(pr, lax.rem(pc + k, n_pcol))

    @pl.when(home != pr)
    def _():
        for k in range(n_pcol):
            greet(home, lax.rem(pc + k, n_pcol))

    def place(r):
        return r * n_prow + pr

    def load(g, h, r):
        return pltpu.make_async_copy(
            factor.at[per_level * g + r, 0, h, 0],
            tiles.at[g, place(r)] if g == h else own.at[pair(g, h), r],
            load_sem.at[pair(g, h), r],
        )

    flat_copy = pltpu.make_async_copy(right.at[:, 0], flat, flat_sem)
    flat_copy.start()
    for g in range(levels):
        for h in range(g + 1):
            for r in range(per_level):
                load(g, h, r).start()

    ends = []
    for g in range(levels):
        base = 2 ** (levels - 1 - g) - 1
        total, ends_now = jnp.int32(0), []
        for k in range(base + 1):
            total = total + nodes[base + k]
            ends_now.append(total)
        ends.append(ends_now)

    def node(g, i):
        found = jnp.int32(2 ** (levels - 1 - g) - 1)
        for end in ends[g][:-1]:
            found = found + jnp.where(i >= end, 1, 0)
        return found

    col_node = [node(g, pc) for g in range(levels)]

    def diag_bit(g, i):
        return jnp.where((node(g, i) == col_node[g]) & (i >= pc), 1.0, 0.0).astype(jnp.float32)

    def front_bit(g, h, i):
        return front[col_node[h], g * n_pcol + i].astype(jnp.float32)

    def live(i, action):
        pl.when(i >= pc)(action)

    def tile_copies(g, r):
        i = place(r)
        targets = [lax.rem(pr + 2 * k, n_prow) for k in range(1, pairs + 1)] + [near]
        return [
            remote(factor.at[per_level * g + r, 0, g, 0], tiles.at[g, i],
                   tile_send.at[g, r, k], tile_recv.at[g, i], target, pc)
            for k, target in enumerate(targets)
        ]

    def relay_copies(g, r):
        copies = []
        for k in range(1, pairs + 1):
            i = r * n_prow + lax.rem(pr + 2 * k, n_prow)
            copies.append((i, remote(tiles.at[g, i], tiles.at[g, i], relay_send.at[g, r, k - 1],
                                     tile_recv.at[g, i], near, pc)))
        return copies

    def issue(g):
        for r in range(per_level):
            def go(r=r):
                for copy in tile_copies(g, r):
                    copy.start()
            live(place(r), go)

    def relay(g):
        for r in range(per_level):
            for i, copy in relay_copies(g, r):
                def go(i=i, copy=copy):
                    arrived(tiles.at[g, i], tile_recv.at[g, i])
                    copy.start()
                live(i, go)

    def collect(g):
        for r in range(per_level):
            load(g, g, r).wait()
            for k in range(pairs + 1):
                i = r * n_prow + lax.rem(near + 2 * k, n_prow)
                live(i, lambda i=i: arrived(tiles.at[g, i], tile_recv.at[g, i]))

    def settle(g):
        for r in range(per_level):
            def go(r=r):
                for copy in tile_copies(g, r):
                    copy.wait_send()
            live(place(r), go)
            for i, copy in relay_copies(g, r):
                live(i, copy.wait_send)

    far = [lax.rem(pc // n_prow + 1 + k, per_level) for k in range(per_level)]

    def row_sends(p, ch, r):
        copies = []
        for k in range(n_prow):
            s = lax.rem(pr + k, n_prow)
            copy = remote(first.at[p % 2, ch, r, s], inbox.at[p, ch, pc], first_send.at[p % 2, ch, r, s],
                          part_recv.at[p, ch, pc], s, place(r))
            copies.append((copy, (place(r) != pc) if k == 0 else None))
        return copies

    def each(copies, action):
        for copy, test in copies:
            if test is None:
                action(copy)
            else:
                pl.when(test)(lambda copy=copy: action(copy))

    def row_products(p, ch):
        g = (p + 1) // 2
        if p == 0:
            x = turned[0].reshape(n_prow, CHUNKS, rows, size)[:, ch]
        else:
            gather(g - 1, ch)
            x = solved[g - 1, :, ch]
        x = x.reshape(n_prow * rows, size)
        for r in far:
            if p == 0:
                value = dot_nt(x, tiles[0, place(r)]) * diag_bit(0, place(r))
            else:
                value = dot_nt(x, own[pair(g, g - 1), r]) * front_bit(g, g - 1, place(r))
            value = value.reshape(n_prow, rows, size)
            if g > 1:
                value = value + acc[g, r, :, ch]
            first[p % 2, ch, r] = value.astype(jnp.bfloat16)
        if p == 0 and ch == 0:
            pl.semaphore_wait(barrier, n_prow - 1 + n_pcol - 1 + (n_prow - 1) * per_level)
        for r in far:
            def go(r=r):
                each(row_sends(p, ch, r), lambda copy: copy.start())

                @pl.when(place(r) == pc)
                def _():
                    inbox[p, ch, pc] = first[p % 2, ch, r, pr]
            if p == 0:
                live(place(r), go)
            else:
                go()

    def row_finish(p, ch):
        for r in far:
            def go(r=r):
                each(row_sends(p, ch, r), lambda copy: copy.wait_send())
            if p == 0:
                live(place(r), go)
            else:
                go()

    def part_copy(p, ch, i):
        return remote(parts.at[p // 2 % 2, ch, i], inbox.at[p, ch, pc], part_send.at[p // 2 % 2, ch, i],
                      part_recv.at[p, ch, pc], pr, i)

    def column_products(p, ch, x):
        g = p // 2

        def batch(base):
            for i in [base + m for m in range(BATCH)]:
                value = dot_nt(x, tiles[g, i]) * diag_bit(g, i)
                parts[p // 2 % 2, ch, i] = value.astype(jnp.bfloat16)

        if n_pcol <= 8:
            for k in range(n_pcol // BATCH - 1, -1, -1):
                batch(k * BATCH)
        else:
            def loop(k, carry):
                batch(k * BATCH)
                return carry

            lax.fori_loop(0, n_pcol // BATCH, loop, 0)

        for i in range(n_pcol - 1, 0, -1):
            pl.when(i > pc)(part_copy(p, ch, i).start)
        inbox[p, ch, pc] = parts[p // 2 % 2, ch, pc]

    def column_finish(p, ch):
        for i in range(n_pcol - 1, 0, -1):
            pl.when(i > pc)(part_copy(p, ch, i).wait_send)

    def by_rows(p):
        return p == 0 or p % 2 == 1

    def finish(p):
        for ch in range(CHUNKS):
            (row_finish if by_rows(p) else column_finish)(p, ch)

    def later(g, h):
        x = solved[h].reshape(width, size)
        for r in range(per_level):
            load(g, h, r).wait()
            value = dot_nt(x, own[pair(g, h), r]) * front_bit(g, h, place(r))
            value = value.reshape(n_prow, CHUNKS, rows, size)
            acc[g, r] = value if h == 0 else acc[g, r] + value

    def share_copies(g, ch):
        return [
            remote(solved.at[g, pr, ch], solved.at[g, pr, ch], share_send.at[g, ch, s],
                   share_recv.at[g, ch, pr], s, pc)
            for s in [lax.rem(pr + k, n_prow) for k in range(1, n_prow)]
        ]

    def reduce(p, ch):
        def add(source, total):
            kept = source == pc
            if by_rows(p):
                kept = kept & (home == pr)
            pl.when(jnp.logical_not(kept))(
                lambda: arrived(inbox.at[p, ch, source], part_recv.at[p, ch, source])
            )
            return total + inbox[p, ch, source].astype(jnp.float32)

        total = jnp.zeros((rows, size), jnp.float32)
        total = lax.fori_loop(0, pc + 1 if p % 2 == 0 else n_pcol, add, total)
        g = (p + 1) // 2
        if p % 2 == 0:
            solved[g, pr, ch] = total.astype(jnp.bfloat16)
            for copy in share_copies(g, ch):
                copy.start()
            return None
        start = pl.multiple_of((pr * CHUNKS + ch) * rows, rows)
        return (turned[g, pl.ds(start, rows), :].astype(jnp.float32) - total).astype(jnp.bfloat16)

    def gather(g, ch):
        for k in range(1, n_prow):
            s = lax.rem(pr + k, n_prow)
            arrived(solved.at[g, s, ch], share_recv.at[g, ch, s])

    def write(g):
        out[g, 0] = solved[g].reshape(width, size).astype(jnp.float32).T.astype(jnp.bfloat16)
        for ch in range(CHUNKS):
            for copy in share_copies(g, ch):
                copy.wait_send()

    def turn(g):
        turned[g] = flat[g].astype(jnp.float32).T.astype(jnp.bfloat16)

    flat_copy.wait()
    turn(0)
    for r in range(per_level):
        load(0, 0, r).wait()
    for p in range(phases):
        g = (p + 1) // 2
        if p % 2 == 1:
            for r in range(per_level):
                load(g, g - 1, r).wait()
        if p > 0 and p % 2 == 0:
            collect(g)
        if p % 2 == 1:
            for ch in range(CHUNKS):
                reduce(p - 1, ch)
        for ch in range(CHUNKS):
            if by_rows(p):
                row_products(p, ch)
            else:
                column_products(p, ch, reduce(p - 1, ch))
        if p == 0:
            issue(1)
            for level in range(1, levels):
                turn(level)
        else:
            finish(p - 1)
        if p % 2 == 1:
            if g + 1 < levels:
                issue(g + 1)
            relay(g)
            if g > 1 and g + 1 < levels:
                for h in range(g - 1):
                    later(g + 1, h)
            write(g - 1)
        elif 0 < g < levels - 1:
            later(g + 1, g - 1)
    finish(phases - 1)
    for g in range(1, levels):
        settle(g)
    for ch in range(CHUNKS):
        reduce(phases - 1, ch)
    for ch in range(CHUNKS):
        gather(levels - 1, ch)
    write(levels - 1)


def local(n_prow, n_pcol, factor, right_side, node_blocks, front_mask):
    levels, _, size, width = right_side.shape
    per_level = n_pcol // n_prow
    rows = width // n_prow // CHUNKS
    phases = 2 * levels - 1
    count = levels * (levels + 1) // 2
    relays = max(1, n_prow // 2 - 1)
    anywhere = pl.BlockSpec(memory_space=pl.ANY)
    smem = pl.BlockSpec(memory_space=pltpu.SMEM)
    dma = pltpu.SemaphoreType.DMA
    bf16 = jnp.bfloat16
    return pl.pallas_call(
        functools.partial(kernel, n_prow, n_pcol),
        out_shape=jax.ShapeDtypeStruct(right_side.shape, bf16),
        in_specs=[anywhere, anywhere, smem, smem],
        out_specs=pl.BlockSpec(memory_space=pltpu.VMEM),
        scratch_shapes=[
            pltpu.VMEM((count, per_level, size, size), bf16),
            pltpu.VMEM((levels, n_pcol, size, size), bf16),
            pltpu.VMEM((levels, size, width), bf16),
            pltpu.VMEM((levels, width, size), bf16),
            pltpu.VMEM((levels, per_level, n_prow, CHUNKS, rows, size), jnp.float32),
            pltpu.VMEM((2, CHUNKS, per_level, n_prow, rows, size), bf16),
            pltpu.VMEM((2, CHUNKS, n_pcol, rows, size), bf16),
            pltpu.VMEM((phases, CHUNKS, n_pcol, rows, size), bf16),
            pltpu.VMEM((levels, n_prow, CHUNKS, rows, size), bf16),
            dma((count, per_level)),
            dma,
            dma((levels, per_level, n_prow // 2)),
            dma((levels, per_level, relays)),
            dma((levels, n_pcol)),
            dma((2, CHUNKS, per_level, n_prow)),
            dma((2, CHUNKS, n_pcol)),
            dma((phases, CHUNKS, n_pcol)),
            dma((levels, CHUNKS, n_prow)),
            dma((levels, CHUNKS, n_prow)),
        ],
        compiler_params=pltpu.CompilerParams(
            collective_id=0, has_side_effects=True, vmem_limit_bytes=60 * 2**20
        ),
    )(factor, right_side, node_blocks, front_mask)


def solution(mesh):
    in_specs = (P(None, "prow", None, "pcol", None, None), P(None, "pcol", None, None), P(), P())
    out_specs = P(None, "pcol", None, None)
    return jax.shard_map(
        functools.partial(local, mesh.shape["prow"], mesh.shape["pcol"]),
        mesh=mesh, in_specs=in_specs, out_specs=out_specs, check_vma=False,
    )
```

```python
import functools

import jax
import jax.numpy as jnp
from jax import lax
from jax.experimental import pallas as pl
from jax.experimental.pallas import tpu as pltpu
from jax.sharding import PartitionSpec as P

MESH = pl.DeviceIdType.MESH
CHUNKS = 4
BATCH = 4


def pair(g, h):
    return g * (g + 1) // 2 + h


def dot_nt(a, b):
    return lax.dot_general(a, b, (((1,), (1,)), ((), ())), preferred_element_type=jnp.float32)


def kernel(
    n_prow, n_pcol, factor, right, nodes, front, out,
    own, tiles, flat, turned, acc, first, parts, inbox, mates, solved,
    load_sem, flat_sem, tile_send, relay_send, tile_recv,
    first_send, part_send, part_recv, mate_send, mate_recv, share_send, share_recv,
):
    levels, _, size, width = right.shape
    per_level = n_pcol // n_prow
    rows = solved.shape[3]
    chunks = solved.shape[2]
    pairs = n_prow // 2 - 1
    phases = 2 * levels - 1
    pr = lax.axis_index("prow")
    pc = lax.axis_index("pcol")
    near = pr + 1 - 2 * lax.rem(pr, 2)
    half = n_pcol // 2
    side = pc // half
    mate = pc + 1 - 2 * lax.rem(pc, 2)
    adds = lax.rem(pc, 2) == lax.rem(pr, 2)

    def device(row, col):
        return {"prow": row, "pcol": col}

    def remote(src, dst, send, recv, row, col):
        return pltpu.make_async_remote_copy(
            src_ref=src, dst_ref=dst, send_sem=send, recv_sem=recv,
            device_id=device(row, col), device_id_type=MESH,
        )

    def arrived(slot, sem):
        remote(slot, slot, share_send.at[0, 0, 0], sem, pr, pc).wait_recv()

    barrier = pltpu.get_barrier_semaphore()
    home = lax.rem(pc, n_prow)

    def greet(row, col):
        pl.semaphore_signal(barrier, inc=1, device_id=device(row, col), device_id_type=MESH)

    for k in range(1, n_prow):
        greet(lax.rem(pr + k, n_prow), pc)
    for k in range(1, n_pcol):
        greet(pr, lax.rem(pc + k, n_pcol))

    @pl.when(home != pr)
    def _():
        for k in range(n_pcol):
            greet(home, lax.rem(pc + k, n_pcol))

    def place(r):
        return r * n_prow + pr

    def load(g, h, r):
        return pltpu.make_async_copy(
            factor.at[per_level * g + r, 0, h, 0],
            tiles.at[g, place(r)] if g == h else own.at[pair(g, h), r],
            load_sem.at[pair(g, h), r],
        )

    flat_copy = pltpu.make_async_copy(right.at[:, 0], flat, flat_sem)
    flat_copy.start()
    for g in range(levels):
        for h in range(g + 1):
            for r in range(per_level):
                load(g, h, r).start()

    ends = []
    for g in range(levels):
        base = 2 ** (levels - 1 - g) - 1
        total, ends_now = jnp.int32(0), []
        for k in range(base + 1):
            total = total + nodes[base + k]
            ends_now.append(total)
        ends.append(ends_now)

    def node(g, i):
        found = jnp.int32(2 ** (levels - 1 - g) - 1)
        for end in ends[g][:-1]:
            found = found + jnp.where(i >= end, 1, 0)
        return found

    col_node = [node(g, pc) for g in range(levels)]

    def diag_bit(g, i):
        return jnp.where((node(g, i) == col_node[g]) & (i >= pc), 1.0, 0.0).astype(jnp.float32)

    def front_bit(g, h, i):
        return front[col_node[h], g * n_pcol + i].astype(jnp.float32)

    def live(i, action):
        pl.when(i >= pc)(action)

    def tile_copies(g, r):
        i = place(r)
        targets = [lax.rem(pr + 2 * k, n_prow) for k in range(1, pairs + 1)] + [near]
        return [
            remote(factor.at[per_level * g + r, 0, g, 0], tiles.at[g, i],
                   tile_send.at[g, r, k], tile_recv.at[g, i], target, pc)
            for k, target in enumerate(targets)
        ]

    def relay_copies(g, r):
        copies = []
        for k in range(1, pairs + 1):
            i = r * n_prow + lax.rem(pr + 2 * k, n_prow)
            copies.append((i, remote(tiles.at[g, i], tiles.at[g, i], relay_send.at[g, r, k - 1],
                                     tile_recv.at[g, i], near, pc)))
        return copies

    def issue(g):
        for r in range(per_level):
            def go(r=r):
                for copy in tile_copies(g, r):
                    copy.start()
            live(place(r), go)

    def relay(g):
        for r in range(per_level):
            for i, copy in relay_copies(g, r):
                def go(i=i, copy=copy):
                    arrived(tiles.at[g, i], tile_recv.at[g, i])
                    copy.start()
                live(i, go)

    def collect(g):
        for r in range(per_level):
            load(g, g, r).wait()
            for k in range(pairs + 1):
                i = r * n_prow + lax.rem(near + 2 * k, n_prow)
                live(i, lambda i=i: arrived(tiles.at[g, i], tile_recv.at[g, i]))

    def settle(g):
        for r in range(per_level):
            def go(r=r):
                for copy in tile_copies(g, r):
                    copy.wait_send()
            live(place(r), go)
            for i, copy in relay_copies(g, r):
                live(i, copy.wait_send)

    few = per_level // 2

    def far_row(m):
        return (1 - side) * few + m

    def near_row(m):
        return side * few + m

    def row_sends(p, ch, r, keep):
        copies = []
        for k in range(n_prow):
            s = lax.rem(pr + k, n_prow)
            copy = remote(first.at[p % 2, ch, r, s], inbox.at[p, ch, pc], first_send.at[p % 2, ch, r, s],
                          part_recv.at[p, ch, pc], s, place(r))
            copies.append((copy, (place(r) != pc) if keep and k == 0 else None))
        return copies

    def each(copies, action):
        for copy, test in copies:
            if test is None:
                action(copy)
            else:
                pl.when(test)(lambda copy=copy: action(copy))

    def row_mate(p, ch, m):
        return remote(first.at[p % 2, ch, far_row(m)], mates.at[p, ch, pl.ds(m * n_prow, n_prow)],
                      mate_send.at[p % 2, ch, m], mate_recv.at[p, ch, m], pr, mate)

    def crosses(p):
        return side == 0 if p % 2 == 0 else side >= 0

    def row_products(p, ch):
        g = (p + 1) // 2
        if p == 0:
            x = turned[0].reshape(n_prow, chunks, rows, size)[:, ch]
        else:
            gather(g - 1, ch)
            x = solved[g - 1, :, ch]
        x = x.reshape(n_prow * rows, size)
        for r in [far_row(m) for m in range(few)] + [near_row(m) for m in range(few)]:
            if p == 0:
                value = dot_nt(x, tiles[0, place(r)]) * diag_bit(0, place(r))
            else:
                value = dot_nt(x, own[pair(g, g - 1), r]) * front_bit(g, g - 1, place(r))
            value = value.reshape(n_prow, rows, size)
            if g > 1:
                value = value + acc[g, r, :, ch]
            first[p % 2, ch, r] = value.astype(jnp.bfloat16)
        if p == 0 and ch == 0:
            pl.semaphore_wait(barrier, n_prow - 1 + n_pcol - 1 + (n_prow - 1) * per_level)
        for m in range(few):
            pl.when(crosses(p) & jnp.logical_not(adds))(row_mate(p, ch, m).start)
        for m in range(few):
            r = near_row(m)

            def go(r=r):
                each(row_sends(p, ch, r, True), lambda copy: copy.start())

                @pl.when(place(r) == pc)
                def _():
                    inbox[p, ch, pc] = first[p % 2, ch, r, pr]
            if p == 0:
                live(place(r), go)
            else:
                go()

    def row_combine(p, ch):
        @pl.when(crosses(p) & adds)
        def _():
            for m in range(few):
                r = far_row(m)
                slot = mates.at[p, ch, pl.ds(m * n_prow, n_prow)]
                arrived(slot, mate_recv.at[p, ch, m])
                total = first[p % 2, ch, r].astype(jnp.float32) + slot[...].astype(jnp.float32)
                first[p % 2, ch, r] = total.astype(jnp.bfloat16)
                each(row_sends(p, ch, r, False), lambda copy: copy.start())

    def row_finish(p, ch):
        for m in range(few):
            r = near_row(m)

            def go(r=r):
                each(row_sends(p, ch, r, True), lambda copy: copy.wait_send())
            if p == 0:
                live(place(r), go)
            else:
                go()
            pl.when(crosses(p) & jnp.logical_not(adds))(row_mate(p, ch, m).wait_send)

            @pl.when(crosses(p) & adds)
            def _():
                each(row_sends(p, ch, far_row(m), False), lambda copy: copy.wait_send())

    def part_copy(p, ch, i):
        return remote(parts.at[p // 2 % 2, ch, i], inbox.at[p, ch, pc], part_send.at[p // 2 % 2, ch, i],
                      part_recv.at[p, ch, pc], pr, i)

    def part_mate(p, ch, m):
        return remote(parts.at[p // 2 % 2, ch, half + 2 * m + lax.rem(mate, 2)], mates.at[p, ch, m],
                      mate_send.at[p % 2, ch, m], mate_recv.at[p, ch, m], pr, mate)

    def column_products(p, ch, x):
        g = p // 2

        def batch(base):
            for i in [base + m for m in range(BATCH)]:
                value = dot_nt(x, tiles[g, i]) * diag_bit(g, i)
                parts[p // 2 % 2, ch, i] = value.astype(jnp.bfloat16)

        if n_pcol <= 8:
            for k in range(n_pcol // BATCH - 1, -1, -1):
                batch(k * BATCH)
        else:
            def loop(k, carry):
                batch(k * BATCH)
                return carry

            lax.fori_loop(0, n_pcol // BATCH, loop, 0)

        @pl.when(side == 0)
        def _():
            for m in range(half // 2):
                part_mate(p, ch, m).start()

        for m in range(half):
            i = side * half + m
            pl.when(i > pc)(part_copy(p, ch, i).start)
        inbox[p, ch, pc] = parts[p // 2 % 2, ch, pc]

    def column_combine(p, ch):
        @pl.when(side == 0)
        def _():
            for m in range(half // 2):
                i = half + 2 * m + lax.rem(pc, 2)
                arrived(mates.at[p, ch, m], mate_recv.at[p, ch, m])
                total = parts[p // 2 % 2, ch, i].astype(jnp.float32) + mates[p, ch, m].astype(jnp.float32)
                parts[p // 2 % 2, ch, i] = total.astype(jnp.bfloat16)
                part_copy(p, ch, i).start()

    def column_finish(p, ch):
        @pl.when(side == 0)
        def _():
            for m in range(half // 2):
                part_mate(p, ch, m).wait_send()
                part_copy(p, ch, half + 2 * m + lax.rem(pc, 2)).wait_send()

        for m in range(half):
            i = side * half + m
            pl.when(i > pc)(part_copy(p, ch, i).wait_send)

    def by_rows(p):
        return p == 0 or p % 2 == 1

    def finish(p):
        for ch in range(chunks):
            (row_finish if by_rows(p) else column_finish)(p, ch)

    def later(g, h):
        x = solved[h].reshape(width, size)
        for r in range(per_level):
            load(g, h, r).wait()
            value = dot_nt(x, own[pair(g, h), r]) * front_bit(g, h, place(r))
            value = value.reshape(n_prow, chunks, rows, size)
            acc[g, r] = value if h == 0 else acc[g, r] + value

    def share_copies(g, ch):
        return [
            remote(solved.at[g, pr, ch], solved.at[g, pr, ch], share_send.at[g, ch, s],
                   share_recv.at[g, ch, pr], s, pc)
            for s in [lax.rem(pr + k, n_prow) for k in range(1, n_prow)]
        ]

    def reduce(p, ch):
        def add(source, total):
            kept = source == pc
            if by_rows(p):
                kept = kept & (home == pr)
            pl.when(jnp.logical_not(kept))(
                lambda: arrived(inbox.at[p, ch, source], part_recv.at[p, ch, source])
            )
            return total + inbox[p, ch, source].astype(jnp.float32)

        total = jnp.zeros((rows, size), jnp.float32)
        near_count = lax.rem(pc, half) + 1 if p % 2 == 0 else half
        far_count = side * (half // 2) if p % 2 == 0 else half // 2
        total = lax.fori_loop(0, near_count, lambda m, t: add(side * half + m, t), total)
        total = lax.fori_loop(
            0, far_count, lambda m, t: add((1 - side) * half + 2 * m + lax.rem(pc, 2), t), total
        )
        g = (p + 1) // 2
        if p % 2 == 0:
            solved[g, pr, ch] = total.astype(jnp.bfloat16)
            for copy in share_copies(g, ch):
                copy.start()
            return None
        start = pl.multiple_of((pr * chunks + ch) * rows, rows)
        return (turned[g, pl.ds(start, rows), :].astype(jnp.float32) - total).astype(jnp.bfloat16)

    def gather(g, ch):
        for k in range(1, n_prow):
            s = lax.rem(pr + k, n_prow)
            arrived(solved.at[g, s, ch], share_recv.at[g, ch, s])

    def write(g):
        out[g] = solved[g].reshape(width, size)
        for ch in range(chunks):
            for copy in share_copies(g, ch):
                copy.wait_send()

    def turn(g):
        turned[g] = flat[g].astype(jnp.float32).T.astype(jnp.bfloat16)

    flat_copy.wait()
    turn(0)
    for r in range(per_level):
        load(0, 0, r).wait()
    for p in range(phases):
        g = (p + 1) // 2
        if p % 2 == 1:
            for r in range(per_level):
                load(g, g - 1, r).wait()
        if p > 0 and p % 2 == 0:
            collect(g)
        if p % 2 == 1:
            for ch in range(chunks):
                reduce(p - 1, ch)
        for ch in range(chunks):
            if by_rows(p):
                row_products(p, ch)
            else:
                column_products(p, ch, reduce(p - 1, ch))
        for ch in range(chunks):
            (row_combine if by_rows(p) else column_combine)(p, ch)
        if p == 0:
            issue(1)
            for level in range(1, levels):
                turn(level)
        else:
            finish(p - 1)
        if p % 2 == 1:
            if g + 1 < levels:
                issue(g + 1)
            relay(g)
            if g > 1 and g + 1 < levels:
                for h in range(g - 1):
                    later(g + 1, h)
            write(g - 1)
        elif 0 < g < levels - 1:
            later(g + 1, g - 1)
    finish(phases - 1)
    for g in range(1, levels):
        settle(g)
    for ch in range(chunks):
        reduce(phases - 1, ch)
    for ch in range(chunks):
        gather(levels - 1, ch)
    write(levels - 1)


def local(n_prow, n_pcol, factor, right_side, node_blocks, front_mask):
    levels, _, size, width = right_side.shape
    per_level = n_pcol // n_prow
    chunks = max(1, min(CHUNKS, width // n_prow // 16))
    rows = width // n_prow // chunks
    phases = 2 * levels - 1
    count = levels * (levels + 1) // 2
    relays = max(1, n_prow // 2 - 1)
    anywhere = pl.BlockSpec(memory_space=pl.ANY)
    smem = pl.BlockSpec(memory_space=pltpu.SMEM)
    dma = pltpu.SemaphoreType.DMA
    bf16 = jnp.bfloat16
    result = pl.pallas_call(
        functools.partial(kernel, n_prow, n_pcol),
        out_shape=jax.ShapeDtypeStruct((levels, width, size), bf16),
        in_specs=[anywhere, anywhere, smem, smem],
        out_specs=pl.BlockSpec(memory_space=pltpu.VMEM),
        scratch_shapes=[
            pltpu.VMEM((count, per_level, size, size), bf16),
            pltpu.VMEM((levels, n_pcol, size, size), bf16),
            pltpu.VMEM((levels, size, width), bf16),
            pltpu.VMEM((levels, width, size), bf16),
            pltpu.VMEM((levels, per_level, n_prow, chunks, rows, size), jnp.float32),
            pltpu.VMEM((2, chunks, per_level, n_prow, rows, size), bf16),
            pltpu.VMEM((2, chunks, n_pcol, rows, size), bf16),
            pltpu.VMEM((phases, chunks, n_pcol, rows, size), bf16),
            pltpu.VMEM((phases, chunks, n_pcol // 2, rows, size), bf16),
            pltpu.VMEM((levels, n_prow, chunks, rows, size), bf16),
            dma((count, per_level)),
            dma,
            dma((levels, per_level, n_prow // 2)),
            dma((levels, per_level, relays)),
            dma((levels, n_pcol)),
            dma((2, chunks, per_level, n_prow)),
            dma((2, chunks, n_pcol)),
            dma((phases, chunks, n_pcol)),
            dma((2, chunks, n_pcol // 2)),
            dma((phases, chunks, n_pcol // 2)),
            dma((levels, chunks, n_prow)),
            dma((levels, chunks, n_prow)),
        ],
        compiler_params=pltpu.CompilerParams(
            collective_id=0, has_side_effects=True, vmem_limit_bytes=60 * 2**20
        ),
    )(factor, right_side, node_blocks, front_mask)
    return jnp.swapaxes(result, 1, 2)[:, None]


def solution(mesh):
    in_specs = (P(None, "prow", None, "pcol", None, None), P(None, "pcol", None, None), P(), P())
    out_specs = P(None, "pcol", None, None)
    return jax.shard_map(
        functools.partial(local, mesh.shape["prow"], mesh.shape["pcol"]),
        mesh=mesh, in_specs=in_specs, out_specs=out_specs, check_vma=False,
    )
```

```python
import functools

import jax
import jax.numpy as jnp
from jax import lax
from jax.experimental import pallas as pl
from jax.experimental.pallas import tpu as pltpu
from jax.sharding import PartitionSpec as P

MESH = pl.DeviceIdType.MESH
CHUNKS = 2
BATCH = 4


def pair(g, h):
    return g * (g + 1) // 2 + h


def dot_nt(a, b):
    return lax.dot_general(a, b, (((1,), (1,)), ((), ())), preferred_element_type=jnp.float32)


def kernel(
    n_prow, n_pcol, factor, right, nodes, front, out,
    own, tiles, flat, turned, acc, first, parts, inbox, mates, solved,
    load_sem, flat_sem, tile_send, relay_send, tile_recv,
    first_send, part_send, part_recv, mate_send, mate_recv, share_send, share_recv,
):
    levels, _, size, width = right.shape
    per_level = n_pcol // n_prow
    rows = solved.shape[3]
    chunks = solved.shape[2]
    pairs = n_prow // 2 - 1
    phases = 2 * levels - 1
    pr = lax.axis_index("prow")
    pc = lax.axis_index("pcol")
    near = pr + 1 - 2 * lax.rem(pr, 2)
    half = n_pcol // 2
    side = pc // half
    mate = pc + 1 - 2 * lax.rem(pc, 2)
    adds = lax.rem(pc, 2) == lax.rem(pr, 2)

    def device(row, col):
        return {"prow": row, "pcol": col}

    def remote(src, dst, send, recv, row, col):
        return pltpu.make_async_remote_copy(
            src_ref=src, dst_ref=dst, send_sem=send, recv_sem=recv,
            device_id=device(row, col), device_id_type=MESH,
        )

    def arrived(slot, sem):
        remote(slot, slot, share_send.at[0, 0, 0], sem, pr, pc).wait_recv()

    barrier = pltpu.get_barrier_semaphore()
    home = lax.rem(pc, n_prow)

    def greet(row, col):
        pl.semaphore_signal(barrier, inc=1, device_id=device(row, col), device_id_type=MESH)

    for k in range(1, n_prow):
        greet(lax.rem(pr + k, n_prow), pc)
    for k in range(1, n_pcol):
        greet(pr, lax.rem(pc + k, n_pcol))

    @pl.when(home != pr)
    def _():
        for k in range(n_pcol):
            greet(home, lax.rem(pc + k, n_pcol))

    def place(r):
        return r * n_prow + pr

    def load(g, h, r):
        return pltpu.make_async_copy(
            factor.at[per_level * g + r, 0, h, 0],
            tiles.at[g, place(r)] if g == h else own.at[pair(g, h), r],
            load_sem.at[pair(g, h), r],
        )

    flat_copy = pltpu.make_async_copy(right.at[:, 0], flat, flat_sem)
    flat_copy.start()
    for g in range(levels):
        for h in range(g + 1):
            for r in range(per_level):
                load(g, h, r).start()

    ends = []
    for g in range(levels):
        base = 2 ** (levels - 1 - g) - 1
        total, ends_now = jnp.int32(0), []
        for k in range(base + 1):
            total = total + nodes[base + k]
            ends_now.append(total)
        ends.append(ends_now)

    def node(g, i):
        found = jnp.int32(2 ** (levels - 1 - g) - 1)
        for end in ends[g][:-1]:
            found = found + jnp.where(i >= end, 1, 0)
        return found

    col_node = [node(g, pc) for g in range(levels)]

    def diag_bit(g, i):
        return jnp.where((node(g, i) == col_node[g]) & (i >= pc), 1.0, 0.0).astype(jnp.float32)

    def front_bit(g, h, i):
        return front[col_node[h], g * n_pcol + i].astype(jnp.float32)

    def live(i, action):
        pl.when(i >= pc)(action)

    def tile_copies(g, r):
        i = place(r)
        targets = [lax.rem(pr + 2 * k, n_prow) for k in range(1, pairs + 1)] + [near]
        return [
            remote(factor.at[per_level * g + r, 0, g, 0], tiles.at[g, i],
                   tile_send.at[g, r, k], tile_recv.at[g, i], target, pc)
            for k, target in enumerate(targets)
        ]

    def relay_copies(g, r):
        copies = []
        for k in range(1, pairs + 1):
            i = r * n_prow + lax.rem(pr + 2 * k, n_prow)
            copies.append((i, remote(tiles.at[g, i], tiles.at[g, i], relay_send.at[g, r, k - 1],
                                     tile_recv.at[g, i], near, pc)))
        return copies

    def issue(g):
        for r in range(per_level):
            def go(r=r):
                for copy in tile_copies(g, r):
                    copy.start()
            live(place(r), go)

    def relay(g):
        for r in range(per_level):
            for i, copy in relay_copies(g, r):
                def go(i=i, copy=copy):
                    arrived(tiles.at[g, i], tile_recv.at[g, i])
                    copy.start()
                live(i, go)

    def collect(g):
        for r in range(per_level):
            load(g, g, r).wait()
            for k in range(pairs + 1):
                i = r * n_prow + lax.rem(near + 2 * k, n_prow)
                live(i, lambda i=i: arrived(tiles.at[g, i], tile_recv.at[g, i]))

    def settle(g):
        for r in range(per_level):
            def go(r=r):
                for copy in tile_copies(g, r):
                    copy.wait_send()
            live(place(r), go)
            for i, copy in relay_copies(g, r):
                live(i, copy.wait_send)

    few = per_level // 2

    def far_row(m):
        return (1 - side) * few + m

    def near_row(m):
        return side * few + m

    def row_sends(p, ch, r, keep):
        copies = []
        for k in range(n_prow):
            s = lax.rem(pr + k, n_prow)
            copy = remote(first.at[p % 2, ch, r, s], inbox.at[p, ch, pc], first_send.at[p % 2, ch, r, s],
                          part_recv.at[p, ch, pc], s, place(r))
            copies.append((copy, (place(r) != pc) if keep and k == 0 else None))
        return copies

    def each(copies, action):
        for copy, test in copies:
            if test is None:
                action(copy)
            else:
                pl.when(test)(lambda copy=copy: action(copy))

    def row_mate(p, ch, m):
        return remote(first.at[p % 2, ch, far_row(m)], mates.at[p, ch, pl.ds(m * n_prow, n_prow)],
                      mate_send.at[p % 2, ch, m], mate_recv.at[p, ch, m], pr, mate)

    def crosses(p):
        return side == 0 if p % 2 == 0 else side >= 0

    def row_products(p, ch):
        g = (p + 1) // 2
        if p == 0:
            x = turned[0].reshape(n_prow, chunks, rows, size)[:, ch]
        else:
            gather(g - 1, ch)
            x = solved[g - 1, :, ch]
        x = x.reshape(n_prow * rows, size)
        for r in [far_row(m) for m in range(few)] + [near_row(m) for m in range(few)]:
            if p == 0:
                value = dot_nt(x, tiles[0, place(r)]) * diag_bit(0, place(r))
            else:
                value = dot_nt(x, own[pair(g, g - 1), r]) * front_bit(g, g - 1, place(r))
            value = value.reshape(n_prow, rows, size)
            if g > 1:
                value = value + acc[g, r, :, ch]
            first[p % 2, ch, r] = value.astype(jnp.bfloat16)
        if p == 0 and ch == 0:
            pl.semaphore_wait(barrier, n_prow - 1 + n_pcol - 1 + (n_prow - 1) * per_level)
        for m in range(few):
            pl.when(crosses(p) & jnp.logical_not(adds))(row_mate(p, ch, m).start)
        for m in range(few):
            r = near_row(m)

            def go(r=r):
                each(row_sends(p, ch, r, True), lambda copy: copy.start())

                @pl.when(place(r) == pc)
                def _():
                    inbox[p, ch, pc] = first[p % 2, ch, r, pr]
            if p == 0:
                live(place(r), go)
            else:
                go()

    def row_combine(p, ch):
        @pl.when(crosses(p) & adds)
        def _():
            for m in range(few):
                r = far_row(m)
                slot = mates.at[p, ch, pl.ds(m * n_prow, n_prow)]
                arrived(slot, mate_recv.at[p, ch, m])
                total = first[p % 2, ch, r].astype(jnp.float32) + slot[...].astype(jnp.float32)
                first[p % 2, ch, r] = total.astype(jnp.bfloat16)
                each(row_sends(p, ch, r, False), lambda copy: copy.start())

    def row_finish(p, ch):
        for m in range(few):
            r = near_row(m)

            def go(r=r):
                each(row_sends(p, ch, r, True), lambda copy: copy.wait_send())
            if p == 0:
                live(place(r), go)
            else:
                go()
            pl.when(crosses(p) & jnp.logical_not(adds))(row_mate(p, ch, m).wait_send)

            @pl.when(crosses(p) & adds)
            def _():
                each(row_sends(p, ch, far_row(m), False), lambda copy: copy.wait_send())

    def part_copy(p, ch, i):
        return remote(parts.at[p // 2 % 2, ch, i], inbox.at[p, ch, pc], part_send.at[p // 2 % 2, ch, i],
                      part_recv.at[p, ch, pc], pr, i)

    def part_mate(p, ch, m):
        return remote(parts.at[p // 2 % 2, ch, half + 2 * m + lax.rem(mate, 2)], mates.at[p, ch, m],
                      mate_send.at[p % 2, ch, m], mate_recv.at[p, ch, m], pr, mate)

    def column_products(p, ch, x):
        g = p // 2

        def batch(base):
            for i in [base + m for m in range(BATCH)]:
                value = dot_nt(x, tiles[g, i]) * diag_bit(g, i)
                parts[p // 2 % 2, ch, i] = value.astype(jnp.bfloat16)

        if n_pcol <= 8:
            for k in range(n_pcol // BATCH - 1, -1, -1):
                batch(k * BATCH)
        else:
            def loop(k, carry):
                batch(k * BATCH)
                return carry

            lax.fori_loop(0, n_pcol // BATCH, loop, 0)

        @pl.when(side == 0)
        def _():
            for m in range(half // 2):
                part_mate(p, ch, m).start()

        for m in range(half):
            i = side * half + m
            pl.when(i > pc)(part_copy(p, ch, i).start)
        inbox[p, ch, pc] = parts[p // 2 % 2, ch, pc]

    def column_combine(p, ch):
        @pl.when(side == 0)
        def _():
            for m in range(half // 2):
                i = half + 2 * m + lax.rem(pc, 2)
                arrived(mates.at[p, ch, m], mate_recv.at[p, ch, m])
                total = parts[p // 2 % 2, ch, i].astype(jnp.float32) + mates[p, ch, m].astype(jnp.float32)
                parts[p // 2 % 2, ch, i] = total.astype(jnp.bfloat16)
                part_copy(p, ch, i).start()

    def column_finish(p, ch):
        @pl.when(side == 0)
        def _():
            for m in range(half // 2):
                part_mate(p, ch, m).wait_send()
                part_copy(p, ch, half + 2 * m + lax.rem(pc, 2)).wait_send()

        for m in range(half):
            i = side * half + m
            pl.when(i > pc)(part_copy(p, ch, i).wait_send)

    def by_rows(p):
        return p == 0 or p % 2 == 1

    def finish(p):
        for ch in range(chunks):
            (row_finish if by_rows(p) else column_finish)(p, ch)

    def later(g, h):
        x = solved[h].reshape(width, size)
        for r in range(per_level):
            load(g, h, r).wait()
            value = dot_nt(x, own[pair(g, h), r]) * front_bit(g, h, place(r))
            value = value.reshape(n_prow, chunks, rows, size)
            acc[g, r] = value if h == 0 else acc[g, r] + value

    def share_copies(g, ch):
        return [
            remote(solved.at[g, pr, ch], solved.at[g, pr, ch], share_send.at[g, ch, s],
                   share_recv.at[g, ch, pr], s, pc)
            for s in [lax.rem(pr + k, n_prow) for k in range(1, n_prow)]
        ]

    def reduce(p, ch):
        sources = []
        for m in range(half):
            source = side * half + m
            sources.append((source, source <= pc if p % 2 == 0 else None))
        for m in range(half // 2):
            source = (1 - side) * half + 2 * m + lax.rem(pc, 2)
            sources.append((source, side == 1 if p % 2 == 0 else None))
        for k, (source, test) in enumerate(sources):
            slot, sem = inbox.at[p, ch, source], part_recv.at[p, ch, source]
            if k < half:
                kept = source == pc
                if by_rows(p):
                    kept = kept & (home == pr)
                moved = jnp.logical_not(kept)
                test = moved if test is None else test & moved
            if test is None:
                arrived(slot, sem)
            else:
                pl.when(test)(lambda slot=slot, sem=sem: arrived(slot, sem))
        total = None
        for source, test in sources:
            value = inbox[p, ch, source].astype(jnp.float32)
            if test is not None:
                value = jnp.where(test, value, 0.0)
            total = value if total is None else total + value
        g = (p + 1) // 2
        if p % 2 == 0:
            solved[g, pr, ch] = total.astype(jnp.bfloat16)
            for copy in share_copies(g, ch):
                copy.start()
            return None
        start = pl.multiple_of((pr * chunks + ch) * rows, rows)
        return (turned[g, pl.ds(start, rows), :].astype(jnp.float32) - total).astype(jnp.bfloat16)

    def gather(g, ch):
        for k in range(1, n_prow):
            s = lax.rem(pr + k, n_prow)
            arrived(solved.at[g, s, ch], share_recv.at[g, ch, s])

    def write(g):
        out[g] = solved[g].reshape(width, size)
        for ch in range(chunks):
            for copy in share_copies(g, ch):
                copy.wait_send()

    def turn(g):
        turned[g] = flat[g].astype(jnp.float32).T.astype(jnp.bfloat16)

    flat_copy.wait()
    turn(0)
    for r in range(per_level):
        load(0, 0, r).wait()
    for p in range(phases):
        g = (p + 1) // 2
        if p % 2 == 1:
            for r in range(per_level):
                load(g, g - 1, r).wait()
        if p > 0 and p % 2 == 0:
            collect(g)
        if p % 2 == 1:
            for ch in range(chunks):
                reduce(p - 1, ch)
        for ch in range(chunks):
            if by_rows(p):
                row_products(p, ch)
            else:
                column_products(p, ch, reduce(p - 1, ch))
        for ch in range(chunks):
            (row_combine if by_rows(p) else column_combine)(p, ch)
        if p == 0:
            issue(1)
            for level in range(1, levels):
                turn(level)
        else:
            finish(p - 1)
        if p % 2 == 1:
            if g + 1 < levels:
                issue(g + 1)
            relay(g)
            if g > 1 and g + 1 < levels:
                for h in range(g - 1):
                    later(g + 1, h)
            write(g - 1)
        elif 0 < g < levels - 1:
            later(g + 1, g - 1)
    finish(phases - 1)
    for g in range(1, levels):
        settle(g)
    for ch in range(chunks):
        reduce(phases - 1, ch)
    for ch in range(chunks):
        gather(levels - 1, ch)
    write(levels - 1)


def local(n_prow, n_pcol, factor, right_side, node_blocks, front_mask):
    levels, _, size, width = right_side.shape
    per_level = n_pcol // n_prow
    chunks = max(1, min(CHUNKS, width // n_prow // 16))
    rows = width // n_prow // chunks
    phases = 2 * levels - 1
    count = levels * (levels + 1) // 2
    relays = max(1, n_prow // 2 - 1)
    anywhere = pl.BlockSpec(memory_space=pl.ANY)
    smem = pl.BlockSpec(memory_space=pltpu.SMEM)
    dma = pltpu.SemaphoreType.DMA
    bf16 = jnp.bfloat16
    result = pl.pallas_call(
        functools.partial(kernel, n_prow, n_pcol),
        out_shape=jax.ShapeDtypeStruct((levels, width, size), bf16),
        in_specs=[anywhere, anywhere, smem, smem],
        out_specs=pl.BlockSpec(memory_space=pltpu.VMEM),
        scratch_shapes=[
            pltpu.VMEM((count, per_level, size, size), bf16),
            pltpu.VMEM((levels, n_pcol, size, size), bf16),
            pltpu.VMEM((levels, size, width), bf16),
            pltpu.VMEM((levels, width, size), bf16),
            pltpu.VMEM((levels, per_level, n_prow, chunks, rows, size), jnp.float32),
            pltpu.VMEM((2, chunks, per_level, n_prow, rows, size), bf16),
            pltpu.VMEM((2, chunks, n_pcol, rows, size), bf16),
            pltpu.VMEM((phases, chunks, n_pcol, rows, size), bf16),
            pltpu.VMEM((phases, chunks, n_pcol // 2, rows, size), bf16),
            pltpu.VMEM((levels, n_prow, chunks, rows, size), bf16),
            dma((count, per_level)),
            dma,
            dma((levels, per_level, n_prow // 2)),
            dma((levels, per_level, relays)),
            dma((levels, n_pcol)),
            dma((2, chunks, per_level, n_prow)),
            dma((2, chunks, n_pcol)),
            dma((phases, chunks, n_pcol)),
            dma((2, chunks, n_pcol // 2)),
            dma((phases, chunks, n_pcol // 2)),
            dma((levels, chunks, n_prow)),
            dma((levels, chunks, n_prow)),
        ],
        compiler_params=pltpu.CompilerParams(
            collective_id=0, has_side_effects=True, vmem_limit_bytes=60 * 2**20
        ),
    )(factor, right_side, node_blocks, front_mask)
    return jnp.swapaxes(result, 1, 2)[:, None]


def solution(mesh):
    in_specs = (P(None, "prow", None, "pcol", None, None), P(None, "pcol", None, None), P(), P())
    out_specs = P(None, "pcol", None, None)
    return jax.shard_map(
        functools.partial(local, mesh.shape["prow"], mesh.shape["pcol"]),
        mesh=mesh, in_specs=in_specs, out_specs=out_specs, check_vma=False,
    )
```
